32 devices in a mesh: expert: 8 (over y, x, core), context: 4 (over z).
Axes of the slice: x: 2, y: 2, z: 4, core: 2. Of those that a mesh axis runs over, the one named last changes fastest.
Arguments:
- tokens: bfloat16 [8192, 768], P(('expert', 'context')), may hold values from -6 to 6
- gain_attn: float32 [768], replicated, may hold values from 0.5 to 1.5
- w_query: bfloat16 [768, 768], replicated, may hold values from -0.21875 to 0.21875
- w_key: bfloat16 [768, 768], replicated, may hold values from -0.21875 to 0.21875
- w_value: bfloat16 [768, 768], replicated, may hold values from -0.21875 to 0.21875
- w_proj: bfloat16 [768, 768], replicated, may hold values from -3 to 3
- bias_table: float32 [32, 12], replicated, may hold values from -4 to 4
- gain_moe: float32 [768], replicated, may hold values from 0.5 to 1.5
- w_router: bfloat16 [768, 8], replicated, may hold values from -0.15625 to 0.15625
- w_up: bfloat16 [8, 768, 3072], P('expert'), may hold values from -0.21875 to 0.21875
- w_down: bfloat16 [8, 3072, 768], P('expert'), may hold values from -0.109375 to 0.109375
- routes: int32 [8192, 2], P(('expert', 'context')), may hold values from 0 to 7, all different within a row; in each aligned block of 256 rows (0 to 255, 256 to 511, ...) at most 128 rows name the same one
- bucket_ids: int32 [1024], replicated, may hold values from 0 to 31, as said below
- cotangent: bfloat16 [8192, 768], P(('expert', 'context')), may hold values from -6 to 6
Outputs:
- output: bfloat16 [8192, 768], P(('expert', 'context'))
- grad_tokens: bfloat16 [8192, 768], P(('expert', 'context'))
- grad_gain_attn: float32 [768], replicated
- grad_query: float32 [768, 768], replicated
- grad_key: float32 [768, 768], replicated
- grad_value: float32 [768, 768], replicated
- grad_proj: float32 [768, 768], replicated
- grad_table: float32 [32, 12], replicated
- grad_gain_moe: float32 [768], replicated
- grad_router: float32 [768, 8], replicated
- grad_up: float32 [8, 768, 3072], P('expert', None, 'context')
- grad_down: float32 [8, 3072, 768], P('expert', 'context')
The draws below stay inside these ranges and needn't reach their ends.
Inputs may be any that keep to these rules, and one draw needn't show every extreme that they name: `routes`: in each aligned block of 256 rows (the rows of one device) no expert is named by more than 128 rows, a bound that some block reaches; the 2 experts of a row differ. `bucket_ids`: entry d is the bucket of a key d positions before its query; the entries never fall, rise by at most one from one distance to the next, entry 0 is 0 and the last entry is 31.
All inputs are finite; a program needn't handle non-finite values.
Results may differ from the reference program's by a relative error of at most 0.02.
Values may be sent and summed in bfloat16 or wider, within the bound.
No kernel may reach another device: no remote copies, remote signals or barrier semaphores. Data moves between devices by JAX's collectives and lax.ppermute only.
A program may use at most 192 MiB of HBM per device.

```python
import math
import jax
import jax.numpy as jnp
import numpy as np
from jax import lax

D = 768
HEADS = 12
HEAD = 64
FF = 3072
TOP = 2
BUCKETS = 32
TOK_DEV = 256
SEQ = 1024
TOKENS = 8192
EXPERTS = 8
CAP = 128
N_EXPERT = 8
N_CONTEXT = 4


def draw_bucket_ids(key, part):
    key = jax.random.fold_in(key, 7)
    bounds = jax.random.permutation(key, SEQ - 1)[:BUCKETS - 1] + 1
    distance = jnp.arange(SEQ, dtype=jnp.int32)
    return jnp.sum((distance[:, None] >= bounds[None, :]).astype(jnp.int32), axis=1).astype(jnp.int32)


def block_scale(rng, shape, split, least, top_value):
    def one(dim, shards_of):
        heights = jax.random.uniform(jax.random.fold_in(jax.random.fold_in(rng, 6), dim), (shards_of,), jnp.float32, least / len(split), top_value / len(split))
        return jnp.repeat(jnp.exp(heights), shape[dim] // shards_of).reshape((-1,) + (1,) * (len(shape) - dim - 1))

    loudness = one(*split[0])
    for cut in split[1:]:
        loudness = loudness * one(*cut)
    return loudness


def deal_out(own_key, own, number, rows, number_of, top, limit, skew):
    ranking = jax.random.permutation(own_key, number_of)
    packed, common = load_shares(number_of, rows * top, limit, skew, True), load_shares(number_of, rows * top, limit, skew, False)
    places = jnp.arange(number_of)

    def named(sizes, offset_by):
        used = int((sizes > 0).sum())
        fixed = max(1, used // 4)
        shifted = fixed + (places - fixed + offset_by * (used - fixed)) % max(1, number_of - fixed)
        return jnp.zeros((number_of,), jnp.int32).at[ranking[jnp.where(places < fixed, places, shifted)]].set(jnp.asarray(sizes, jnp.int32))

    sizes = jnp.where(number % 4 == 0, named(packed, number // 4), named(common, number - number // 4 - 1))
    mixed = jax.random.permutation(jax.random.fold_in(own, 3), number_of)
    source_of, taker = mixed[0:number_of // 2 * 2:2], mixed[1:number_of // 2 * 2:2]
    margin = jnp.minimum(sizes[source_of] - 1, limit - sizes[taker]) // 2
    margin = jnp.where((source_of == ranking[0]) | (taker == ranking[0]) | (sizes[taker] == 0), 0, jnp.maximum(margin, 0))
    shifted = jax.random.randint(jax.random.fold_in(own, 4), (number_of // 2,), 0, 1 << 20) % (margin + 1)
    sizes = sizes.at[source_of].add(-shifted).at[taker].add(shifted)
    labels = jnp.searchsorted(jnp.cumsum(sizes), jnp.arange(rows * top), side="right").astype(jnp.int32)
    grid = labels.reshape(top, rows).T
    grid = grid[jax.random.permutation(jax.random.fold_in(own, 1), rows)]
    offset_by = jax.random.randint(jax.random.fold_in(own, 2), (rows, 1), 0, top)
    return jnp.take_along_axis(grid, (jnp.arange(top)[None, :] + offset_by) % top, axis=1)


def load_shares(amount, total, limit, slope, full):
    weights = [(1 << 20) // math.isqrt(grade ** slope) + 1 for grade in range(1, amount + 1)]
    largest = limit if full else min(limit, max(-(-total // amount), total * weights[0] // sum(weights)))
    least = 1 if total - largest >= amount - 1 else 0
    holding, spare = [largest] + [least] * (amount - 1), total - largest - least * (amount - 1)
    while spare > 0:
        free = [i for i in range(1, amount) if holding[i] < largest] or [i for i in range(1, amount) if holding[i] < limit]
        mass, budget = sum([weights[i] for i in free]), spare
        for i in free:
            extra = min(limit - holding[i], max(1, budget * weights[i] // mass), spare)
            holding[i] = holding[i] + extra
            spare = spare - extra
    return np.array(holding)


def normal_values(stream_key, dims, spread, limit, split=(), held_as=jnp.bfloat16):
    loudness = block_scale(stream_key, dims, split, -0.22, 0.18) if split else 1.0
    result = jax.random.normal(stream_key, dims, jnp.float32) * spread * loudness
    return jnp.minimum(jnp.maximum(result, -limit), limit).astype(held_as)


def setup_inputs(seed: int = 0) -> dict:
    arg_keys = jax.random.split(jax.random.key(seed), 15)
    tokens = normal_values(arg_keys[0], (TOKENS, D), 1.0, 6.0, ((0, 32),))
    gain_attn = jnp.clip(1.0 + 0.1 * jax.random.normal(arg_keys[1], (D,), jnp.float32), 0.5, 1.5)
    w_query = normal_values(arg_keys[2], (D, D), D ** -0.5, 0.21875)
    w_key = normal_values(arg_keys[3], (D, D), D ** -0.5, 0.21875)
    w_value = normal_values(arg_keys[4], (D, D), D ** -0.5, 0.21875)
    w_proj = normal_values(arg_keys[5], (D, D), 4 ** -0.5, 3.0)
    bias_table = normal_values(arg_keys[6], (BUCKETS, HEADS), 1.0, 4.0, (), jnp.float32)
    gain_moe = jnp.clip(1.0 + 0.1 * jax.random.normal(arg_keys[7], (D,), jnp.float32), 0.5, 1.5)
    w_router = normal_values(arg_keys[8], (D, EXPERTS), (2 * D) ** -0.5, 0.15625)
    w_up = normal_values(arg_keys[9], (EXPERTS, D, FF), D ** -0.5, 0.21875, ((0, 8),))
    w_down = normal_values(arg_keys[10], (EXPERTS, FF, D), FF ** -0.5, 0.109375, ((0, 8),))
    routes_keys = jax.random.split(jax.random.fold_in(arg_keys[11], 1), TOKENS // TOK_DEV)
    routes_turns = jax.random.permutation(jax.random.fold_in(arg_keys[11], 3), TOKENS // TOK_DEV)
    routes = jax.vmap(lambda own, number: deal_out(jax.random.fold_in(arg_keys[11], 2), own, number, TOK_DEV, EXPERTS, TOP, CAP, 2))(routes_keys, routes_turns).reshape((TOKENS, TOP))
    bucket_ids = draw_bucket_ids(jax.random.fold_in(arg_keys[14], 71), 0)
    cotangent = normal_values(arg_keys[13], (TOKENS, D), 1.0, 6.0, ((0, 32),))
    return {"tokens": tokens, "gain_attn": gain_attn, "w_query": w_query, "w_key": w_key, "w_value": w_value, "w_proj": w_proj, "bias_table": bias_table, "gain_moe": gain_moe, "w_router": w_router, "w_up": w_up, "w_down": w_down, "routes": routes, "bucket_ids": bucket_ids, "cotangent": cotangent}


EPSILON = 1e-06
HIGHEST = lax.Precision.HIGHEST
MASKED = -1000000000.0

@jax.custom_vjp
def low(v):
    return lax.optimization_barrier(v.astype(jnp.bfloat16)).astype(jnp.float32)

@jax.custom_vjp
def low_back(v):
    return v

def low_keep(v):
    return (low(v), None)

def low_pass(kept, grad):
    return (grad,)

def back_keep(v):
    return (v, None)

def back_low(kept, grad):
    return (low(grad),)
low.defvjp(low_keep, low_pass)
low_back.defvjp(back_keep, back_low)

def product(left, right):
    return jnp.dot(left, right, precision=HIGHEST)

def rms_norm(value, gain):
    return value * lax.rsqrt(lax.optimization_barrier(jnp.mean(value * value, axis=-1, keepdims=True)) + EPSILON) * gain

def slot_positions(routes):
    blocks = routes.reshape(N_EXPERT * N_CONTEXT, TOK_DEV * TOP)
    member = (blocks[:, :, None] == jnp.arange(EXPERTS, dtype=jnp.int32)[None, None, :]).astype(jnp.int32)
    earlier = jnp.cumsum(member, axis=1) - member
    local = lax.optimization_barrier(jnp.sum(earlier * member, axis=2))
    offset = jnp.arange(N_EXPERT * N_CONTEXT, dtype=jnp.int32)[:, None] * CAP
    return (local + offset).reshape(TOKENS, TOP).astype(jnp.int32)

def attend(normed, w_query, w_key, w_value, bias_table, bucket_ids):
    length = normed.shape[0]
    query = low_back(low(product(normed, w_query))).reshape(length, HEADS, HEAD)
    keys = low_back(low(product(normed, w_key))).reshape(length, HEADS, HEAD)
    values = low_back(low(product(normed, w_value))).reshape(length, HEADS, HEAD)
    raw = low_back(jnp.einsum('qhd,khd->hqk', query, keys, precision=HIGHEST) * HEAD ** (-0.5))
    places = jnp.arange(length, dtype=jnp.int32)
    distance = places[:, None] - places[None, :]
    bucket = jnp.take(bucket_ids, jnp.maximum(distance, 0), axis=0)
    bias = jnp.transpose(jnp.take(bias_table, bucket, axis=0), (2, 0, 1))
    scores = jnp.where(distance[None] >= 0, raw + bias, MASKED)
    weights = low(jax.nn.softmax(scores, axis=-1))
    mixed = low_back(low(jnp.einsum('hqk,khd->qhd', weights, values, precision=HIGHEST)))
    return mixed.reshape(length, HEADS * HEAD)

def expert_apply(pieces):
    rows_in, upper, lower = pieces
    hidden = low_back(product(rows_in, upper))
    active = low(jax.nn.gelu(hidden, approximate=False))
    return low(low_back(product(active, lower)))

def forward(tokens, gain_attn, w_query, w_key, w_value, w_proj, bias_table, gain_moe, w_router, w_up, w_down, routes, slots, bucket_ids):
    normed = low(rms_norm(tokens, gain_attn))
    sequences = normed.reshape(N_EXPERT, SEQ, D)

    def one_sequence(part):
        return attend(part, w_query, w_key, w_value, bias_table, bucket_ids)
    mixed = lax.map(jax.checkpoint(one_sequence), sequences).reshape(TOKENS, D)
    middle = tokens + low_back(product(mixed, w_proj))
    routed = low(rms_norm(middle, gain_moe))
    logits = product(routed, w_router)
    gates = jax.nn.softmax(jnp.take_along_axis(logits, routes, axis=1), axis=-1)
    buffer = jnp.zeros((EXPERTS, N_EXPERT * N_CONTEXT * CAP, D), jnp.float32)
    buffer = buffer.at[routes.reshape(-1), slots.reshape(-1)].set(jnp.repeat(routed, TOP, axis=0))
    expert_out = lax.map(jax.checkpoint(expert_apply), (low_back(buffer), w_up, w_down))
    picked = expert_out[routes, slots]
    return middle + lax.optimization_barrier(jnp.sum(gates[:, :, None] * picked, axis=1))

def reference(tokens, gain_attn, w_query, w_key, w_value, w_proj, bias_table, gain_moe, w_router, w_up, w_down, routes, bucket_ids, cotangent):
    slots = slot_positions(routes)
    floats = tuple((value.astype(jnp.float32) for value in (tokens, gain_attn, w_query, w_key, w_value, w_proj, bias_table, gain_moe, w_router, w_up, w_down)))

    def apply(tokens_in, gain_first, query_weight, key_weight, value_weight, proj_weight, table, gain_second, router_weight, upper, lower):
        return forward(tokens_in, gain_first, query_weight, key_weight, value_weight, proj_weight, table, gain_second, router_weight, upper, lower, routes, slots, bucket_ids)
    output, pullback = jax.vjp(apply, *floats)
    gradients = pullback(cotangent.astype(jnp.float32))
    return (output.astype(jnp.bfloat16), gradients[0].astype(jnp.bfloat16), gradients[1], gradients[2], gradients[3], gradients[4], gradients[5], gradients[6], gradients[7], gradients[8], gradients[9], gradients[10])
```

```python
from functools import partial

import jax
import jax.numpy as jnp
from jax import lax
from jax.experimental import pallas as pl
from jax.experimental.pallas import tpu as pltpu
from jax.sharding import PartitionSpec as P

HEADS = 12
EPSILON = 1e-06
HIGHEST = lax.Precision.HIGHEST
MASKED = -1000000000.0
F32 = jnp.float32
BF16 = jnp.bfloat16
VMEM_LIMIT = 56 * 1024 * 1024
FF_TILE = 512
SPARE = 8


def dot(left, right, dims=((1,), (0,))):
    return lax.dot_general(left, right, (dims, ((), ())), preferred_element_type=F32)


def normalize(value, gain):
    scale = lax.rsqrt(jnp.mean(value * value, axis=1, keepdims=True) + EPSILON)
    return (value * scale * gain, scale)


def normalize_back(grad, value, scale, gain):
    normal = value * scale
    inner = grad * gain
    gain_grad = jnp.sum(grad * normal, axis=0)
    value_grad = scale * (inner - normal * jnp.mean(inner * normal, axis=1, keepdims=True))
    return (value_grad, gain_grad)


def shift(value, axis, step):
    count = lax.axis_size(axis)
    return lax.ppermute(value, axis, [(i, (i + step) % count) for i in range(count)])


def swap(value, axis, bit):
    count = lax.axis_size(axis)
    return lax.ppermute(value, axis, [(i, i ^ bit) for i in range(count)])


def ring_gather(value, axis):
    count = lax.axis_size(axis)
    here = lax.axis_index(axis)
    size = value.shape[0]
    parts = [(0, value)]
    right = left = value
    for step in range(1, count // 2 + 1):
        right = shift(right, axis, 1)
        parts.append((step, right))
        if step <= (count - 1) // 2:
            left = shift(left, axis, -1)
            parts.append((count - step, left))
    whole = jnp.zeros((count * size,) + value.shape[1:], value.dtype)
    for step, part in parts:
        whole = lax.dynamic_update_slice_in_dim(
            whole, part, lax.rem(here - step + count, count) * size, 0
        )
    return whole


def bit_orders(count):
    bits = [1 << i for i in range(count.bit_length() - 1)]
    return bits[:1] + bits[:0:-1]


def halve_sum(value, axis, bits):
    here = lax.axis_index(axis)
    for bit in bits:
        pair = value.reshape((2, value.shape[0] // 2) + value.shape[1:])
        mine = lax.rem(here // bit, 2)
        kept = lax.dynamic_index_in_dim(pair, mine, 0, keepdims=False)
        sent = lax.dynamic_index_in_dim(pair, 1 - mine, 0, keepdims=False)
        value = (kept.astype(F32) + swap(sent, axis, bit).astype(F32)).astype(value.dtype)
    return value[0]


def double_gather(value, axis, bits):
    here = lax.axis_index(axis)
    value = value[None]
    for bit in bits[::-1]:
        other = swap(value, axis, bit)
        first = lax.rem(here // bit, 2) == 0
        value = jnp.concatenate(
            [jnp.where(first, value, other), jnp.where(first, other, value)], axis=0
        )
    return value


def attend_kernel(tokens, gain, weight, bias, normed, qkv, mixed, exact, log_total, tiles):
    length = tokens.shape[0]
    count, size, tile = mixed.shape

    @pl.when(pl.program_id(0) == 0)
    def _():
        def body(i, carry):
            part = pl.ds(i * tile, tile)
            normal, unused = normalize(tokens[part, :].astype(F32), gain[...])
            normed[part, :] = normal.astype(BF16)
            return carry

        lax.fori_loop(0, count, body, 0)

    weight_all = weight[...].reshape(3 * size, weight.shape[2])
    key_parts = []
    for i in range(count):
        part = dot(weight_all, normed[i * tile : (i + 1) * tile, :], ((1,), (1,)))
        low = part.astype(BF16)
        for j in range(3):
            qkv[j, :, i * tile : (i + 1) * tile] = low[j * size : (j + 1) * size, :]
        key_parts.append(part[size : 2 * size, :].T.astype(BF16))
        wide = jnp.broadcast_to(bias[0, :, i * tile : (i + 2) * tile], (tile, 2 * tile))
        turned = pltpu.roll(wide, tile, 1, stride=1, stride_axis=0)
        tiles[(count - 1 - i) * tile : (count - i) * tile, :] = turned[:, :tile]
    keys = jnp.concatenate(key_parts, axis=0)
    factor = size ** (-0.5)
    for i in range(count):
        cols = slice(i * tile, (i + 1) * tile)
        many = (i + 1) * tile
        scores = dot(keys[:many], qkv[0, :, cols]) * factor + tiles[length - many :, :]
        peak = jnp.max(scores, axis=0, keepdims=True)
        weights = jnp.exp(scores - peak)
        total = jnp.sum(weights, axis=0, keepdims=True)
        result = dot(qkv[2, :, :many], weights.astype(BF16)) * (1.0 / total)
        exact[0, :, cols] = result
        mixed[i, :, :] = result.astype(BF16)
        log_total[0, :, cols] = peak + jnp.log(total)


def fold(grid):
    tile = grid.shape[0]
    value = jnp.concatenate([jnp.zeros_like(grid), grid], axis=1)
    half = tile // 2
    while half >= 8:
        value = value[:half] + pltpu.roll(value[half:], 2 * tile - half, 1)
        half //= 2
    return value


def attend_back_kernel(
    qkv, normed, bias, log_total, exact, grads_in, grads, weight_grads, diagonals,
    tiles, sums, keys_acc, values_acc, query_acc,
):
    count, size, tile = grads_in.shape
    factor = size ** (-0.5)
    queries, values, outs, deltas = [], [], [], []
    keys = []
    for i in range(count):
        cols = slice(i * tile, (i + 1) * tile)
        queries.append(qkv[0, :, cols].astype(F32).T.astype(BF16))
        keys.append(qkv[1, :, cols].astype(F32).T.astype(BF16))
        values.append(qkv[2, :, cols].astype(F32).T.astype(BF16))
        out = grads_in[i].astype(F32)
        outs.append(out.T.astype(BF16))
        deltas.append(jnp.sum(out * exact[0, :, cols], axis=0, keepdims=True))
        wide = jnp.broadcast_to(bias[0, :, i * tile : (i + 2) * tile], (tile, 2 * tile))
        turned = pltpu.roll(wide, tile, 1, stride=1, stride_axis=0)
        tiles[i] = turned[:, :tile]
    for d in range(count):
        for j in range(count - d):
            i = j + d
            cols = slice(i * tile, (i + 1) * tile)
            scores = dot(keys[j], qkv[0, :, cols]) * factor + tiles[d]
            probs = jnp.exp(scores - log_total[0, :, cols])
            prob_grads = dot(values[j], grads_in[i])
            score_grads = probs * (prob_grads - deltas[i])
            low = score_grads.astype(BF16)
            value_part = dot(probs.astype(BF16), outs[i])
            key_part = dot(low, queries[i])
            query_part = dot(qkv[1, :, j * tile : (j + 1) * tile], low)
            if j == 0:
                sums[...] = score_grads
            else:
                sums[...] += score_grads
            if d == 0:
                values_acc[j] = value_part
                keys_acc[j] = key_part
                query_acc[i] = query_part
            else:
                values_acc[j] += value_part
                keys_acc[j] += key_part
                query_acc[i] += query_part
        rows = fold(sums[...])
        line = rows[0:1]
        for r in range(1, 8):
            line = line + pltpu.roll(rows[r : r + 1], 2 * tile - r, 1)
        if d == 0:
            diagonals[0, :, : 2 * tile] = line
        else:
            diagonals[0, :, d * tile : (d + 1) * tile] += line[:, :tile]
            diagonals[0, :, (d + 1) * tile : (d + 2) * tile] = line[:, tile:]
    total = None
    for i in range(count):
        query_part = (query_acc[i] * factor).astype(BF16)
        key_part = (keys_acc[i] * factor).T.astype(BF16)
        value_part = values_acc[i].T.astype(BF16)
        grads[i, 0] = query_part
        grads[i, 1] = key_part
        grads[i, 2] = value_part
        stacked = jnp.concatenate([query_part, key_part, value_part], axis=0)
        part = dot(stacked, normed[i * tile : (i + 1) * tile, :])
        total = part if total is None else total + part
    for j in range(3):
        weight_grads[j] = total[j * size : (j + 1) * size, :].astype(BF16)


def expert_kernel(rows_in, out_grads, up, down, active, hidden_grads, row_grads, gate_sums, acc):
    step = pl.program_id(0)
    hidden = dot(rows_in[...], up[...])
    active_grads = dot(out_grads[...], down[...], ((1,), (1,)))
    below = 0.5 * (1.0 + lax.erf(hidden * (0.5**0.5)))
    density = jnp.exp(-0.5 * hidden * hidden) * 0.3989422804014327
    low_active = (hidden * below).astype(BF16)
    active[...] = low_active
    low_grads = (active_grads * (below + hidden * density)).astype(BF16)
    hidden_grads[...] = low_grads
    part = dot(low_grads, up[...], ((1,), (1,)))
    sums = jnp.sum(low_active.astype(F32) * active_grads, axis=1, keepdims=True)

    @pl.when(step == 0)
    def _():
        acc[...] = part
        gate_sums[...] = sums

    @pl.when(step > 0)
    def _():
        acc[...] += part
        gate_sums[...] += sums

    @pl.when(step == pl.num_programs(0) - 1)
    def _():
        row_grads[...] = acc[...].astype(BF16)


def params():
    return pltpu.CompilerParams(
        dimension_semantics=("arbitrary",), vmem_limit_bytes=VMEM_LIMIT
    )


def attend(tokens, gain, weight, bias, count):
    length, width = tokens.shape
    group = bias.shape[0]
    size = weight.shape[1] // group
    tile = length // count
    return pl.pallas_call(
        attend_kernel,
        grid=(group,),
        in_specs=[
            pl.BlockSpec((length, width), lambda h: (0, 0)),
            pl.BlockSpec((1, width), lambda h: (0, 0)),
            pl.BlockSpec((3, size, width), lambda h: (0, h, 0)),
            pl.BlockSpec((1, 1, length + tile), lambda h: (h, 0, 0)),
        ],
        out_specs=[
            pl.BlockSpec((length, width), lambda h: (0, 0)),
            pl.BlockSpec((3, size, length), lambda h: (0, h, 0)),
            pl.BlockSpec((count, size, tile), lambda h: (0, h, 0)),
            pl.BlockSpec((1, size, length), lambda h: (h, 0, 0)),
            pl.BlockSpec((1, 1, length), lambda h: (h, 0, 0)),
        ],
        out_shape=[
            jax.ShapeDtypeStruct((length, width), BF16),
            jax.ShapeDtypeStruct((3, group * size, length), BF16),
            jax.ShapeDtypeStruct((count, group * size, tile), BF16),
            jax.ShapeDtypeStruct((group, size, length), F32),
            jax.ShapeDtypeStruct((group, 1, length), F32),
        ],
        scratch_shapes=[pltpu.VMEM((length, tile), F32)],
        compiler_params=params(),
        name="attend",
    )(tokens, gain, weight, bias)


def attend_back(qkv, normed, bias, log_total, exact, grads_in):
    length, width = normed.shape
    count, _, tile = grads_in.shape
    group, size, _ = exact.shape
    return pl.pallas_call(
        attend_back_kernel,
        grid=(group,),
        in_specs=[
            pl.BlockSpec((3, size, length), lambda h: (0, h, 0)),
            pl.BlockSpec((length, width), lambda h: (0, 0)),
            pl.BlockSpec((1, 1, length + tile), lambda h: (h, 0, 0)),
            pl.BlockSpec((1, 1, length), lambda h: (h, 0, 0)),
            pl.BlockSpec((1, size, length), lambda h: (h, 0, 0)),
            pl.BlockSpec((count, size, tile), lambda h: (0, h, 0)),
        ],
        out_specs=[
            pl.BlockSpec((count, 3, size, tile), lambda h: (0, 0, h, 0)),
            pl.BlockSpec((3, size, width), lambda h: (0, h, 0)),
            pl.BlockSpec((1, 1, length + tile), lambda h: (h, 0, 0)),
        ],
        out_shape=[
            jax.ShapeDtypeStruct((count, 3, group * size, tile), BF16),
            jax.ShapeDtypeStruct((3, group * size, width), BF16),
            jax.ShapeDtypeStruct((group, 1, length + tile), F32),
        ],
        scratch_shapes=[
            pltpu.VMEM((count, tile, tile), F32),
            pltpu.VMEM((tile, tile), F32),
            pltpu.VMEM((count, tile, size), F32),
            pltpu.VMEM((count, tile, size), F32),
            pltpu.VMEM((count, size, tile), F32),
        ],
        compiler_params=params(),
        name="attend_back",
    )(qkv, normed, bias, log_total, exact, grads_in)


def expert(rows_in, out_grads, up, down):
    rows, width = rows_in.shape
    hidden = up.shape[1]
    return pl.pallas_call(
        expert_kernel,
        grid=(hidden // FF_TILE,),
        in_specs=[
            pl.BlockSpec((rows, width), lambda f: (0, 0)),
            pl.BlockSpec((rows, width), lambda f: (0, 0)),
            pl.BlockSpec((width, FF_TILE), lambda f: (0, f)),
            pl.BlockSpec((FF_TILE, width), lambda f: (f, 0)),
        ],
        out_specs=[
            pl.BlockSpec((rows, FF_TILE), lambda f: (0, f)),
            pl.BlockSpec((rows, FF_TILE), lambda f: (0, f)),
            pl.BlockSpec((rows, width), lambda f: (0, 0)),
            pl.BlockSpec((rows, 1), lambda f: (0, 0)),
        ],
        out_shape=[
            jax.ShapeDtypeStruct((rows, hidden), BF16),
            jax.ShapeDtypeStruct((rows, hidden), BF16),
            jax.ShapeDtypeStruct((rows, width), BF16),
            jax.ShapeDtypeStruct((rows, 1), F32),
        ],
        scratch_shapes=[pltpu.VMEM((rows, width), F32)],
        compiler_params=params(),
        name="expert",
    )(rows_in, out_grads, up, down)


def chosen_softmax(logits, chosen, axis):
    peak = jnp.max(jnp.where(chosen, logits, -jnp.inf), axis=axis, keepdims=True)
    peak = jnp.where(peak > -jnp.inf, peak, 0.0)
    parts = jnp.where(chosen, jnp.exp(jnp.where(chosen, logits, peak) - peak), 0.0)
    total = jnp.sum(parts, axis=axis, keepdims=True)
    return parts / jnp.where(total > 0.0, total, 1.0)


def to_experts(value):
    return lax.all_to_all(value, "expert", split_axis=0, concat_axis=0)


def to_context(value):
    return lax.all_to_all(value, "context", split_axis=0, concat_axis=0)


def shards(
    tokens,
    gain_attn,
    w_query,
    w_key,
    w_value,
    w_proj,
    bias_table,
    gain_moe,
    w_router,
    w_up,
    w_down,
    routes,
    bucket_ids,
    cotangent,
):
    rows, width = tokens.shape
    size = width // HEADS
    experts = w_router.shape[1]
    buckets = bias_table.shape[0]
    picks = routes.shape[1]
    capacity = 2 * rows * picks // experts
    slots = experts * capacity
    count = lax.axis_size("context")
    lanes = lax.axis_size("expert")
    here = lax.axis_index("context")
    own = lax.axis_index("expert")
    length = rows * count
    group = -(-HEADS // count)
    held = group * size
    extra = count * group - HEADS

    sequence = ring_gather(tokens, "context")

    expert_ids = jnp.arange(experts, dtype=jnp.int32)
    chosen = jnp.any(routes[:, :, None] == expert_ids[None, None, :], axis=1)
    member = chosen.astype(BF16)
    order = jnp.arange(rows, dtype=jnp.int32)
    earlier = (order[:, None] > order[None, :]).astype(BF16)
    place = dot(earlier, member).astype(jnp.int32)
    dispatch = (
        (place[:, :, None] == jnp.arange(capacity, dtype=jnp.int32)[None, None, :])
        & chosen[:, :, None]
    ).astype(BF16)
    dispatch = dispatch.reshape(rows, slots)

    upstream_slots = to_experts(
        dot(dispatch, cotangent, ((0,), (0,))).astype(BF16).reshape(experts, capacity, width)
    ).reshape(slots, width)
    choices = dot(member, dispatch, ((0,), (0,))).astype(BF16)
    choices = jnp.transpose(choices.reshape(experts, experts, capacity), (1, 0, 2))
    choices = jnp.transpose(to_experts(choices), (1, 0, 2)) > 0.5

    def head_rows(weight):
        whole = jnp.pad(weight, ((0, 0), (0, extra * size)))
        return lax.dynamic_slice_in_dim(whole, here * held, held, 1).T

    head_weights = jnp.stack([head_rows(w) for w in (w_query, w_key, w_value)])
    bucket_match = (
        bucket_ids[:, None] == jnp.arange(buckets, dtype=jnp.int32)[None, :]
    ).astype(F32)
    per_distance = lax.dot_general(
        jnp.pad(bias_table, ((0, 0), (0, extra))), bucket_match, (((0,), (1,)), ((), ())),
        precision=HIGHEST,
    )
    bias = jnp.pad(
        lax.dynamic_slice_in_dim(per_distance, here * group, group, 0),
        ((0, 0), (rows, 0)),
        constant_values=MASKED,
    )[:, None, :]
    normed, qkv, mixed_parts, exact, log_total = attend(
        sequence, gain_attn[None, :], head_weights, bias, count
    )
    mixed = to_context(mixed_parts).reshape(count * held, rows)[:width]
    source = tokens.astype(F32)
    middle = source + dot(mixed, w_proj, ((0,), (0,)))
    moe_normal, moe_scale = normalize(middle, gain_moe)
    routed = moe_normal.astype(BF16)

    received = to_experts(
        dot(dispatch, routed, ((0,), (0,))).astype(BF16).reshape(experts, capacity, width)
    ).reshape(slots, width)
    slot_logits = dot(w_router, received, ((0,), (1,))).reshape(experts, lanes, capacity)
    slot_gates = chosen_softmax(slot_logits, choices, 0)
    slot_gate = lax.dynamic_index_in_dim(slot_gates, own, 0, keepdims=False).reshape(slots, 1)
    out_grads = (slot_gate * upstream_slots.astype(F32)).astype(BF16)
    active, hidden_grads, row_grads, gate_sums = expert(received, out_grads, w_up[0], w_down[0])
    row_returns = to_experts(row_grads.reshape(experts, capacity, width)).reshape(slots, width)
    gate_returns = to_experts(gate_sums.reshape(experts, capacity))
    expert_out = dot(active, w_down[0]).astype(BF16)
    out_returns = to_experts(expert_out.reshape(experts, capacity, width)).reshape(slots, width)
    up_part = dot(received, hidden_grads, ((0,), (0,))).astype(BF16)
    down_part = dot(active, out_grads, ((0,), (0,))).astype(BF16)
    up_grad = lax.psum_scatter(up_part, "context", scatter_dimension=1, tiled=True).astype(F32)
    down_grad = lax.psum_scatter(down_part, "context", scatter_dimension=0, tiled=True).astype(F32)

    logits = dot(routed, w_router)
    gates = chosen_softmax(logits, chosen, 1)
    spread = dispatch.reshape(rows, experts, capacity).astype(F32)
    gated = (spread * gates[:, :, None]).reshape(rows, slots)
    output = middle + jnp.dot(gated, out_returns.astype(F32), precision=HIGHEST)
    weighted = jnp.sum(spread * gate_returns[None], axis=2)
    logit_grads = jnp.where(
        chosen, weighted - gates * jnp.sum(weighted, axis=1, keepdims=True), 0.0
    )
    router_grad = lax.dot_general(
        logit_grads, routed.astype(F32), (((0,), (0,)), ((), ())), precision=HIGHEST
    )
    routed_grads = dot(dispatch, row_returns) + lax.dot_general(
        logit_grads, w_router.astype(F32), (((1,), (1,)), ((), ())), precision=HIGHEST
    )
    upstream = cotangent.astype(F32)
    middle_norm_grads, gain_moe_grad = normalize_back(routed_grads, middle, moe_scale, gain_moe)
    middle_grads = upstream + middle_norm_grads
    branch_grads = middle_grads.astype(BF16)
    mixed_grads = dot(w_proj, branch_grads, ((1,), (1,))).astype(BF16)
    grads_in = to_context(
        jnp.pad(mixed_grads, ((0, extra * size), (0, 0))).reshape(count, held, rows)
    )
    proj_part = jnp.pad(dot(mixed, branch_grads).astype(BF16), ((0, extra * size), (0, 0)))
    proj_rows = jnp.sum(to_context(proj_part.reshape(count, held, width)).astype(F32), axis=0)

    grads_out, weight_grads, diagonals = attend_back(
        qkv, normed, bias, log_total, exact, grads_in
    )
    table_part = jnp.dot(diagonals[:, 0, rows:], bucket_match, precision=HIGHEST)
    table_line = lax.dynamic_update_slice(
        jnp.zeros((count * group, buckets), F32), table_part, (here * group, 0)
    )[:HEADS].reshape(1, HEADS * buckets)
    table_line = jnp.pad(table_line, ((0, 0), (0, width - HEADS * buckets)))
    small = jnp.concatenate([router_grad, gain_moe_grad[None, :], table_line], axis=0)
    small = jnp.pad(small, ((0, lanes * SPARE - small.shape[0]), (0, 0))).astype(BF16)
    chunk = 4 * held // lanes
    pack = jnp.concatenate(
        [
            jnp.concatenate([weight_grads, proj_rows.astype(BF16)[None]], axis=0).reshape(
                lanes, chunk, width
            ),
            small.reshape(lanes, SPARE, width),
        ],
        axis=1,
    )
    bits = bit_orders(lanes)
    pack = halve_sum(pack, "expert", bits)
    pack = ring_gather(pack[None], "context")
    pack = double_gather(pack, "expert", bits)
    whole = jnp.moveaxis(pack[:, :, :chunk], 1, 0).reshape(count, 4, held, width)

    def rows_of(j):
        return whole[:, j].reshape(count * held, width)[:width].astype(F32)

    grad_query, grad_key, grad_value = rows_of(0).T, rows_of(1).T, rows_of(2).T
    grad_proj = rows_of(3)
    small = jnp.sum(pack[:, :, chunk:].astype(F32), axis=1).reshape(lanes * SPARE, width)
    router_total = small[:experts].T
    gain_moe_total = small[experts]
    table_total = small[experts + 1, : HEADS * buckets].reshape(HEADS, buckets).T
    gain_attn_total = (
        jnp.sum(
            grad_query * w_query.astype(F32)
            + grad_key * w_key.astype(F32)
            + grad_value * w_value.astype(F32),
            axis=1,
        )
        / gain_attn
    )

    arrived = to_context(grads_out)
    normed_grads = 0.0
    for j, weight in enumerate((w_query, w_key, w_value)):
        part = arrived[:, j].reshape(count * held, rows)[:width]
        normed_grads = normed_grads + dot(part, weight, ((0,), (1,)))
    attention_scale = lax.rsqrt(jnp.mean(source * source, axis=1, keepdims=True) + EPSILON)
    token_norm_grads, unused = normalize_back(normed_grads, source, attention_scale, gain_attn)
    token_grads = (middle_grads + token_norm_grads).astype(BF16)
    return (
        output.astype(BF16),
        token_grads,
        gain_attn_total,
        grad_query,
        grad_key,
        grad_value,
        grad_proj,
        table_total,
        gain_moe_total,
        router_total,
        up_grad[None],
        down_grad[None],
    )


def solution(mesh):
    return jax.shard_map(
        shards,
        mesh=mesh,
        in_specs=(
            P(("expert", "context"), None),
            P(),
            P(),
            P(),
            P(),
            P(),
            P(),
            P(),
            P(),
            P("expert", None, None),
            P("expert", None, None),
            P(("expert", "context"), None),
            P(),
            P(("expert", "context"), None),
        ),
        out_specs=(
            P(("expert", "context"), None),
            P(("expert", "context"), None),
            P(),
            P(),
            P(),
            P(),
            P(),
            P(),
            P(),
            P(),
            P("expert", None, "context"),
            P("expert", "context", None),
        ),
        check_vma=False,
    )
```

```python
from functools import partial

import jax
import jax.numpy as jnp
from jax import lax
from jax.experimental import pallas as pl
from jax.experimental.pallas import tpu as pltpu
from jax.sharding import PartitionSpec as P

HEADS = 12
EPSILON = 1e-06
HIGHEST = lax.Precision.HIGHEST
MASKED = -1000000000.0
F32 = jnp.float32
BF16 = jnp.bfloat16
VMEM_LIMIT = 56 * 1024 * 1024
FF_TILE = 512
SPARE = 8
ROW_TILE = 512


def dot(left, right, dims=((1,), (0,))):
    return lax.dot_general(left, right, (dims, ((), ())), preferred_element_type=F32)


def normalize(value, gain):
    scale = lax.rsqrt(jnp.mean(value * value, axis=1, keepdims=True) + EPSILON)
    return (value * scale * gain, scale)


def normalize_back(grad, value, scale, gain):
    normal = value * scale
    inner = grad * gain
    gain_grad = jnp.sum(grad * normal, axis=0)
    value_grad = scale * (inner - normal * jnp.mean(inner * normal, axis=1, keepdims=True))
    return (value_grad, gain_grad)


def shift(value, axis, step):
    count = lax.axis_size(axis)
    return lax.ppermute(value, axis, [(i, (i + step) % count) for i in range(count)])


def swap(value, axis, bit):
    count = lax.axis_size(axis)
    return lax.ppermute(value, axis, [(i, i ^ bit) for i in range(count)])


def after(value, *others):
    return lax.optimization_barrier((value, others))[0]


def ring_parts(value, axis, hold=None):
    count = lax.axis_size(axis)
    parts = [(0, value)]
    right = left = value
    for step in range(1, count // 2 + 1):
        if step == 2 and hold is not None:
            right, left = after((right, left), hold)
        right = shift(right, axis, 1)
        parts.append((step, right))
        if step <= (count - 1) // 2:
            left = shift(left, axis, -1)
            parts.append((count - step, left))
    return parts


def in_order(parts, axis):
    count = lax.axis_size(axis)
    here = lax.axis_index(axis)
    value = parts[0][1]
    size = value.shape[0]
    whole = jnp.zeros((count * size,) + value.shape[1:], value.dtype)
    for step, part in parts:
        whole = lax.dynamic_update_slice_in_dim(
            whole, part, lax.rem(here - step + count, count) * size, 0
        )
    return whole


def bit_orders(count):
    bits = [1 << i for i in range(count.bit_length() - 1)]
    return bits[:1] + bits[:0:-1]


def halve_sum(value, axis, bits):
    here = lax.axis_index(axis)
    low = value.dtype
    for bit in bits:
        pair = value.reshape((2, value.shape[0] // 2) + value.shape[1:])
        mine = lax.rem(here // bit, 2)
        kept = lax.dynamic_index_in_dim(pair, mine, 0, keepdims=False)
        sent = lax.dynamic_index_in_dim(pair, 1 - mine, 0, keepdims=False).astype(low)
        value = kept.astype(F32) + swap(sent, axis, bit).astype(F32)
    return value[0]


def double_gather(value, axis, order, bits):
    here = lax.axis_index(axis)
    shape = value.shape
    for bit in order:
        other = swap(value, axis, bit)
        first = lax.rem(here // bit, 2) == 0
        value = jnp.stack([jnp.where(first, value, other), jnp.where(first, other, value)])
    depth = len(order)
    turn = [depth - 1 - order.index(bit) for bit in bits]
    value = jnp.transpose(value, turn + list(range(depth, depth + len(shape))))
    return value.reshape((1 << depth,) + shape)


def attend_kernel(tokens, gain, weight, bias, normed, qkv, mixed, exact, log_total, tiles):
    length = tokens.shape[0]
    count, size, tile = mixed.shape

    @pl.when(pl.program_id(0) == 0)
    def _():
        def body(i, carry):
            part = pl.ds(i * tile, tile)
            normal, unused = normalize(tokens[part, :].astype(F32), gain[...])
            normed[part, :] = normal.astype(BF16)
            return carry

        lax.fori_loop(0, count, body, 0)

    weight_all = weight[...].reshape(3 * size, weight.shape[2])
    key_parts = []
    for i in range(count):
        part = dot(weight_all, normed[i * tile : (i + 1) * tile, :], ((1,), (1,)))
        low = part.astype(BF16)
        for j in range(3):
            qkv[j, :, i * tile : (i + 1) * tile] = low[j * size : (j + 1) * size, :]
        key_parts.append(part[size : 2 * size, :].T.astype(BF16))
        wide = jnp.broadcast_to(bias[0, :, i * tile : (i + 2) * tile], (tile, 2 * tile))
        turned = pltpu.roll(wide, tile, 1, stride=1, stride_axis=0)
        tiles[(count - 1 - i) * tile : (count - i) * tile, :] = turned[:, :tile]
    keys = jnp.concatenate(key_parts, axis=0)
    factor = size ** (-0.5)
    for i in range(count):
        cols = slice(i * tile, (i + 1) * tile)
        many = (i + 1) * tile
        scores = dot(keys[:many], qkv[0, :, cols]) * factor + tiles[length - many :, :]
        peak = jnp.max(scores, axis=0, keepdims=True)
        weights = jnp.exp(scores - peak)
        total = jnp.sum(weights, axis=0, keepdims=True)
        result = dot(qkv[2, :, :many], weights.astype(BF16)) * (1.0 / total)
        exact[0, :, cols] = result
        mixed[i, :, :] = result.astype(BF16)
        log_total[0, :, cols] = peak + jnp.log(total)


def fold(grid):
    tile = grid.shape[0]
    value = jnp.concatenate([jnp.zeros_like(grid), grid], axis=1)
    half = tile // 2
    while half >= 8:
        value = value[:half] + pltpu.roll(value[half:], 2 * tile - half, 1)
        half //= 2
    return value


def attend_back_kernel(
    qkv, normed, bias, log_total, exact, grads_in, grads, weight_grads, diagonals,
    tiles, sums, keys_acc, values_acc, query_acc,
):
    count, size, tile = grads_in.shape
    factor = size ** (-0.5)
    queries, values, outs, deltas = [], [], [], []
    keys = []
    for i in range(count):
        cols = slice(i * tile, (i + 1) * tile)
        queries.append(qkv[0, :, cols].astype(F32).T.astype(BF16))
        keys.append(qkv[1, :, cols].astype(F32).T.astype(BF16))
        values.append(qkv[2, :, cols].astype(F32).T.astype(BF16))
        out = grads_in[i].astype(F32)
        outs.append(out.T.astype(BF16))
        deltas.append(jnp.sum(out * exact[0, :, cols], axis=0, keepdims=True))
        wide = jnp.broadcast_to(bias[0, :, i * tile : (i + 2) * tile], (tile, 2 * tile))
        turned = pltpu.roll(wide, tile, 1, stride=1, stride_axis=0)
        tiles[i] = turned[:, :tile]
    for d in range(count):
        for j in range(count - d):
            i = j + d
            cols = slice(i * tile, (i + 1) * tile)
            scores = dot(keys[j], qkv[0, :, cols]) * factor + tiles[d]
            probs = jnp.exp(scores - log_total[0, :, cols])
            prob_grads = dot(values[j], grads_in[i])
            score_grads = probs * (prob_grads - deltas[i])
            low = score_grads.astype(BF16)
            value_part = dot(probs.astype(BF16), outs[i])
            key_part = dot(low, queries[i])
            query_part = dot(qkv[1, :, j * tile : (j + 1) * tile], low)
            if j == 0:
                sums[...] = score_grads
            else:
                sums[...] += score_grads
            if d == 0:
                values_acc[j] = value_part
                keys_acc[j] = key_part
                query_acc[i] = query_part
            else:
                values_acc[j] += value_part
                keys_acc[j] += key_part
                query_acc[i] += query_part
        rows = fold(sums[...])
        line = rows[0:1]
        for r in range(1, 8):
            line = line + pltpu.roll(rows[r : r + 1], 2 * tile - r, 1)
        if d == 0:
            diagonals[0, :, : 2 * tile] = line
        else:
            diagonals[0, :, d * tile : (d + 1) * tile] += line[:, :tile]
            diagonals[0, :, (d + 1) * tile : (d + 2) * tile] = line[:, tile:]
    total = None
    for i in range(count):
        query_part = (query_acc[i] * factor).astype(BF16)
        key_part = (keys_acc[i] * factor).T.astype(BF16)
        value_part = values_acc[i].T.astype(BF16)
        grads[i, 0] = query_part
        grads[i, 1] = key_part
        grads[i, 2] = value_part
        stacked = jnp.concatenate([query_part, key_part, value_part], axis=0)
        part = dot(stacked, normed[i * tile : (i + 1) * tile, :])
        total = part if total is None else total + part
    for j in range(3):
        weight_grads[j] = total[j * size : (j + 1) * size, :].astype(BF16)


def gelu_parts(hidden):
    below = 0.5 * (1.0 + lax.erf(hidden * (0.5**0.5)))
    density = jnp.exp(-0.5 * hidden * hidden) * 0.3989422804014327
    return (hidden * below).astype(BF16), below + hidden * density


def scaled_rows(target, start, gate, upstream):
    lanes, capacity = gate.shape[0], gate.shape[2]
    for i in range(lanes):
        column = jnp.broadcast_to(gate[i], (8, capacity)).T[:, :1]
        grads = column * upstream[i, :capacity, :].astype(F32)
        target[start + i * capacity : start + (i + 1) * capacity, :] = grads.astype(BF16)


def expert_kernel(rows_in, upstream, gate, up, down, active, row_grads, out_grads, acc, sums):
    step = pl.program_id(0)
    lanes, capacity = gate.shape[0], gate.shape[2]

    @pl.when(step == 0)
    def _():
        scaled_rows(out_grads, 0, gate, upstream)
        acc[...] = jnp.zeros_like(acc)
        sums[...] = jnp.zeros_like(sums)

    hidden = dot(rows_in[...], up[...])
    active_grads = dot(out_grads[...], down[...], ((1,), (1,)))
    low_active, slope = gelu_parts(hidden)
    active[...] = low_active
    low_grads = (active_grads * slope).astype(BF16)
    acc[...] += dot(low_grads, up[...], ((1,), (1,)))
    weighted = low_active.astype(F32) * active_grads
    part = weighted[:, :128]
    for i in range(1, weighted.shape[1] // 128):
        part = part + weighted[:, i * 128 : (i + 1) * 128]
    sums[...] += part

    @pl.when(step == pl.num_programs(0) - 1)
    def _():
        low = acc[...].astype(BF16)
        for i in range(lanes):
            rows = slice(i * capacity, (i + 1) * capacity)
            row_grads[i, :capacity, :] = low[rows, :]
            line = jnp.sum(sums[rows, :].T, axis=0, keepdims=True)
            high = line.astype(BF16).astype(F32)
            both = jnp.concatenate([high, line - high, jnp.zeros((SPARE - 2, capacity), F32)])
            row_grads[i, capacity:, :] = jnp.zeros((SPARE, row_grads.shape[2]), BF16)
            row_grads[i, capacity:, :capacity] = both.astype(BF16)


def expert_grads_kernel(
    index, own_rows, other_rows, own_upstream, other_upstream, own_gate, other_gate, up, down,
    up_grad, down_grad, turned, out_grads, active, hidden_grads,
):
    half = own_rows.shape[0]
    tile = min(ROW_TILE, half)

    @pl.when(pl.program_id(0) == 0)
    def _():
        scaled_rows(out_grads, 0, own_gate, own_upstream)
        scaled_rows(out_grads, half, other_gate, other_upstream)
        for start in range(0, half, tile):
            rows = slice(start, start + tile)
            turned[:, rows] = own_rows[rows, :].T
            turned[:, half + start : half + start + tile] = other_rows[rows, :].T

    for base, source in ((0, own_rows), (half, other_rows)):
        for start in range(0, half, tile):
            rows = slice(base + start, base + start + tile)
            hidden = dot(source[start : start + tile, :], up[...])
            active_grads = dot(out_grads[rows, :], down[...], ((1,), (1,)))
            low_active, slope = gelu_parts(hidden)
            active[rows, :] = low_active
            hidden_grads[rows, :] = (active_grads * slope).astype(BF16)
    up_grad[0] = dot(turned[...], hidden_grads[...]).astype(BF16)
    down_grad[0] = dot(active[...], out_grads[...], ((0,), (0,))).astype(BF16)


def params():
    return pltpu.CompilerParams(
        dimension_semantics=("arbitrary",), vmem_limit_bytes=VMEM_LIMIT
    )


def cost(flops, size):
    return pl.CostEstimate(flops=flops, bytes_accessed=size, transcendentals=0)


def attend(tokens, gain, weight, bias, count):
    length, width = tokens.shape
    group = bias.shape[0]
    size = weight.shape[1] // group
    tile = length // count
    return pl.pallas_call(
        attend_kernel,
        grid=(group,),
        in_specs=[
            pl.BlockSpec((length, width), lambda h: (0, 0)),
            pl.BlockSpec((1, width), lambda h: (0, 0)),
            pl.BlockSpec((3, size, width), lambda h: (0, h, 0)),
            pl.BlockSpec((1, 1, length + tile), lambda h: (h, 0, 0)),
        ],
        out_specs=[
            pl.BlockSpec((length, width), lambda h: (0, 0)),
            pl.BlockSpec((3, size, length), lambda h: (0, h, 0)),
            pl.BlockSpec((count, size, tile), lambda h: (0, h, 0)),
            pl.BlockSpec((1, size, length), lambda h: (h, 0, 0)),
            pl.BlockSpec((1, 1, length), lambda h: (h, 0, 0)),
        ],
        out_shape=[
            jax.ShapeDtypeStruct((length, width), BF16),
            jax.ShapeDtypeStruct((3, group * size, length), BF16),
            jax.ShapeDtypeStruct((count, group * size, tile), BF16),
            jax.ShapeDtypeStruct((group, size, length), F32),
            jax.ShapeDtypeStruct((group, 1, length), F32),
        ],
        scratch_shapes=[pltpu.VMEM((length, tile), F32)],
        compiler_params=params(),
        cost_estimate=cost(14 * length * width * size * group, 8 * length * width),
        name="attend",
    )(tokens, gain, weight, bias)


def attend_back(qkv, normed, bias, log_total, exact, grads_in):
    length, width = normed.shape
    count, _, tile = grads_in.shape
    group, size, _ = exact.shape
    return pl.pallas_call(
        attend_back_kernel,
        grid=(group,),
        in_specs=[
            pl.BlockSpec((3, size, length), lambda h: (0, h, 0)),
            pl.BlockSpec((length, width), lambda h: (0, 0)),
            pl.BlockSpec((1, 1, length + tile), lambda h: (h, 0, 0)),
            pl.BlockSpec((1, 1, length), lambda h: (h, 0, 0)),
            pl.BlockSpec((1, size, length), lambda h: (h, 0, 0)),
            pl.BlockSpec((count, size, tile), lambda h: (0, h, 0)),
        ],
        out_specs=[
            pl.BlockSpec((count, 3, size, tile), lambda h: (0, 0, h, 0)),
            pl.BlockSpec((3, size, width), lambda h: (0, h, 0)),
            pl.BlockSpec((1, 1, length + tile), lambda h: (h, 0, 0)),
        ],
        out_shape=[
            jax.ShapeDtypeStruct((count, 3, group * size, tile), BF16),
            jax.ShapeDtypeStruct((3, group * size, width), BF16),
            jax.ShapeDtypeStruct((group, 1, length + tile), F32),
        ],
        scratch_shapes=[
            pltpu.VMEM((count, tile, tile), F32),
            pltpu.VMEM((tile, tile), F32),
            pltpu.VMEM((count, tile, size), F32),
            pltpu.VMEM((count, tile, size), F32),
            pltpu.VMEM((count, size, tile), F32),
        ],
        compiler_params=params(),
        cost_estimate=cost(18 * length * width * size * group, 8 * length * width),
        name="attend_back",
    )(qkv, normed, bias, log_total, exact, grads_in)


def expert(rows_in, upstream, gate, up, down):
    rows, width = rows_in.shape
    hidden = up.shape[1]
    lanes, _, capacity = gate.shape
    return pl.pallas_call(
        expert_kernel,
        grid=(hidden // FF_TILE,),
        in_specs=[
            pl.BlockSpec((rows, width), lambda f: (0, 0)),
            pl.BlockSpec(upstream.shape, lambda f: (0, 0, 0)),
            pl.BlockSpec(gate.shape, lambda f: (0, 0, 0)),
            pl.BlockSpec((width, FF_TILE), lambda f: (0, f)),
            pl.BlockSpec((FF_TILE, width), lambda f: (f, 0)),
        ],
        out_specs=[
            pl.BlockSpec((rows, FF_TILE), lambda f: (0, f)),
            pl.BlockSpec((lanes, capacity + SPARE, width), lambda f: (0, 0, 0)),
        ],
        out_shape=[
            jax.ShapeDtypeStruct((rows, hidden), BF16),
            jax.ShapeDtypeStruct((lanes, capacity + SPARE, width), BF16),
        ],
        scratch_shapes=[
            pltpu.VMEM((rows, width), BF16),
            pltpu.VMEM((rows, width), F32),
            pltpu.VMEM((rows, 128), F32),
        ],
        compiler_params=params(),
        cost_estimate=cost(8 * rows * width * hidden, 4 * width * hidden),
        name="expert",
    )(rows_in, upstream, gate, up, down)


def expert_grads(index, own_rows, other_rows, own_upstream, other_upstream, own_gate, other_gate, up, down, count):
    half, width = own_rows.shape
    hidden = up.shape[1]
    share = hidden // count
    steps = count // 2
    whole = pl.BlockSpec((half, width), lambda s, i: (0, 0))
    slots = pl.BlockSpec(own_upstream.shape, lambda s, i: (0, 0, 0))
    gates = pl.BlockSpec(own_gate.shape, lambda s, i: (0, 0, 0))
    return pl.pallas_call(
        expert_grads_kernel,
        grid_spec=pltpu.PrefetchScalarGridSpec(
            num_scalar_prefetch=1,
            grid=(steps,),
            in_specs=[
                whole,
                whole,
                slots,
                slots,
                gates,
                gates,
                pl.BlockSpec((width, share), lambda s, i: (0, i[0] + s)),
                pl.BlockSpec((share, width), lambda s, i: (i[0] + s, 0)),
            ],
            out_specs=[
                pl.BlockSpec((1, width, share), lambda s, i: (s, 0, 0)),
                pl.BlockSpec((1, share, width), lambda s, i: (s, 0, 0)),
            ],
            scratch_shapes=[
                pltpu.VMEM((width, 2 * half), BF16),
                pltpu.VMEM((2 * half, width), BF16),
                pltpu.VMEM((2 * half, share), BF16),
                pltpu.VMEM((2 * half, share), BF16),
            ],
        ),
        out_shape=[
            jax.ShapeDtypeStruct((steps, width, share), BF16),
            jax.ShapeDtypeStruct((steps, share, width), BF16),
        ],
        compiler_params=params(),
        cost_estimate=cost(16 * half * width * share * steps, 8 * half * width),
        name="expert_grads",
    )(index, own_rows, other_rows, own_upstream, other_upstream, own_gate, other_gate, up, down)


def chosen_softmax(logits, chosen, axis):
    peak = jnp.max(jnp.where(chosen, logits, -jnp.inf), axis=axis, keepdims=True)
    peak = jnp.where(peak > -jnp.inf, peak, 0.0)
    parts = jnp.where(chosen, jnp.exp(jnp.where(chosen, logits, peak) - peak), 0.0)
    total = jnp.sum(parts, axis=axis, keepdims=True)
    return parts / jnp.where(total > 0.0, total, 1.0)


def to_experts(value):
    return lax.all_to_all(value, "expert", split_axis=0, concat_axis=0)


def to_context(value):
    return lax.all_to_all(value, "context", split_axis=0, concat_axis=0)


def shards(
    tokens,
    gain_attn,
    w_query,
    w_key,
    w_value,
    w_proj,
    bias_table,
    gain_moe,
    w_router,
    w_up,
    w_down,
    routes,
    bucket_ids,
    cotangent,
):
    rows, width = tokens.shape
    size = width // HEADS
    experts = w_router.shape[1]
    buckets = bias_table.shape[0]
    picks = routes.shape[1]
    capacity = 2 * rows * picks // experts
    slots = experts * capacity
    count = lax.axis_size("context")
    lanes = lax.axis_size("expert")
    here = lax.axis_index("context")
    own = lax.axis_index("expert")
    length = rows * count
    group = -(-HEADS // count)
    held = group * size
    extra = count * group - HEADS

    token_parts = ring_parts(tokens, "context")

    expert_ids = jnp.arange(experts, dtype=jnp.int32)
    order = jnp.arange(rows, dtype=jnp.int32)
    earlier = (order[:, None] > order[None, :]).astype(BF16)

    def routing(block):
        chosen = jnp.any(block[:, :, None] == expert_ids[None, None, :], axis=1)
        member = chosen.astype(BF16)
        place = dot(earlier, member).astype(jnp.int32)
        dispatch = (
            (place[:, :, None] == jnp.arange(capacity, dtype=jnp.int32)[None, None, :])
            & chosen[:, :, None]
        ).astype(BF16)
        return chosen, member, dispatch.reshape(rows, slots)

    chosen, member, dispatch = routing(routes)

    def slots_of(dispatch, block):
        sent = dot(dispatch, block, ((0,), (0,))).astype(BF16)
        return sent.reshape(experts, capacity, width)

    def upstream_sent(member, dispatch, block):
        choices = dot(member, dispatch, ((0,), (0,))).astype(BF16)
        choices = jnp.transpose(choices.reshape(experts, experts, capacity), (1, 0, 2))
        choices = jnp.pad(choices, ((0, 0), (0, 0), (0, width - capacity)))
        return jnp.concatenate([slots_of(dispatch, block), choices], axis=1)

    partner = count // 2

    def head_rows(weight):
        whole = jnp.pad(weight, ((0, 0), (0, extra * size)))
        return lax.dynamic_slice_in_dim(whole, here * held, held, 1).T

    head_weights = jnp.stack([head_rows(w) for w in (w_query, w_key, w_value)])

    own_sent, head_weights = after(
        (upstream_sent(member, dispatch, cotangent), head_weights), token_parts[1][1]
    )
    upstream_slots = to_experts(own_sent)
    sequence = in_order(token_parts, "context")
    cotangent_other, routes_other = after((cotangent, routes.T), sequence)
    cotangent_other = swap(cotangent_other, "context", partner)
    routes_other = swap(routes_other, "context", partner)

    bucket_match = (
        bucket_ids[:, None] == jnp.arange(buckets, dtype=jnp.int32)[None, :]
    ).astype(F32)
    per_distance = lax.dot_general(
        jnp.pad(bias_table, ((0, 0), (0, extra))), bucket_match, (((0,), (1,)), ((), ())),
        precision=HIGHEST,
    )
    bias = jnp.pad(
        lax.dynamic_slice_in_dim(per_distance, here * group, group, 0),
        ((0, 0), (rows, 0)),
        constant_values=MASKED,
    )[:, None, :]
    normed, qkv, mixed_parts, exact, log_total = attend(
        sequence, gain_attn[None, :], head_weights, bias, count
    )
    mixed_parts, upstream_slots, cotangent_other, routes_other = lax.optimization_barrier(
        (mixed_parts, upstream_slots, cotangent_other, routes_other)
    )
    unused, member_other, dispatch_other = routing(routes_other.T)
    upstream_other = to_experts(upstream_sent(member_other, dispatch_other, cotangent_other))
    mixed = to_context(mixed_parts).reshape(count * held, rows)[:width]
    source = tokens.astype(F32)
    middle = source + dot(mixed, w_proj, ((0,), (0,)))
    moe_normal, moe_scale = normalize(middle, gain_moe)
    routed = moe_normal.astype(BF16)

    logits = dot(routed, w_router)
    gates = chosen_softmax(logits, chosen, 1)

    def gates_of(received, upstream):
        choices = jnp.moveaxis(upstream[:, capacity:, :capacity], 1, 0) > 0.5
        slot_logits = dot(w_router, received, ((0,), (1,))).reshape(experts, lanes, capacity)
        slot_gates = chosen_softmax(slot_logits, choices, 0)
        return lax.dynamic_index_in_dim(slot_gates, own, 0, keepdims=False)[:, None, :]

    sent, upstream_other = lax.optimization_barrier((slots_of(dispatch, routed), upstream_other))
    received = to_experts(sent).reshape(slots, width)
    routed_other = swap(routed, "context", partner)
    received, routed_other = lax.optimization_barrier((received, routed_other))
    received_other = to_experts(slots_of(dispatch_other, routed_other)).reshape(slots, width)
    slot_gate = gates_of(received, upstream_slots)
    active, row_grads = expert(received, upstream_slots, slot_gate, w_up[0], w_down[0])
    row_grads, received_other = lax.optimization_barrier((row_grads, received_other))
    row_returns = to_experts(row_grads)

    up_part, down_part = expert_grads(
        ((here // partner) * partner)[None],
        received,
        received_other,
        upstream_slots,
        upstream_other,
        slot_gate,
        gates_of(received_other, upstream_other),
        w_up[0],
        w_down[0],
        count,
    )
    row_returns, up_part, down_part = lax.optimization_barrier((row_returns, up_part, down_part))
    low_bits = [1 << i for i in range(partner.bit_length() - 1)][::-1]
    up_grad = halve_sum(up_part, "context", low_bits)
    gate_returns = jnp.sum(row_returns[:, capacity : capacity + 2, :capacity].astype(F32), axis=1)
    row_returns = row_returns[:, :capacity].reshape(slots, width)

    spread = dispatch.reshape(rows, experts, capacity).astype(F32)
    weighted = jnp.sum(spread * gate_returns[None], axis=2)
    logit_grads = jnp.where(
        chosen, weighted - gates * jnp.sum(weighted, axis=1, keepdims=True), 0.0
    )
    router_grad = lax.dot_general(
        logit_grads, routed.astype(F32), (((0,), (0,)), ((), ())), precision=HIGHEST
    )
    routed_grads = dot(dispatch, row_returns) + lax.dot_general(
        logit_grads, w_router.astype(F32), (((1,), (1,)), ((), ())), precision=HIGHEST
    )
    upstream = cotangent.astype(F32)
    middle_norm_grads, gain_moe_grad = normalize_back(routed_grads, middle, moe_scale, gain_moe)
    middle_grads = upstream + middle_norm_grads
    branch_grads = middle_grads.astype(BF16)
    mixed_grads = dot(w_proj, branch_grads, ((1,), (1,))).astype(BF16)
    grads_in = to_context(
        jnp.pad(mixed_grads, ((0, extra * size), (0, 0))).reshape(count, held, rows)
    )
    bits = bit_orders(lanes)
    expert_out = dot(after(active, mixed_grads), w_down[0]).astype(BF16)
    grads_in, expert_out = lax.optimization_barrier((grads_in, expert_out))
    out_returns = to_experts(expert_out.reshape(experts, capacity, width))
    proj_part = dot(mixed, branch_grads).astype(BF16).reshape(lanes, width // lanes, width)
    proj_part = halve_sum(proj_part, "expert", bits).astype(BF16)
    proj_part = to_context(proj_part.reshape(count, width // (lanes * count), width))
    proj_rows = jnp.sum(proj_part.astype(F32), axis=0).astype(BF16)

    grads_out, weight_grads, diagonals = attend_back(
        qkv, normed, bias, log_total, exact, grads_in
    )
    grads_out, weight_grads, out_returns, up_grad = lax.optimization_barrier(
        (grads_out, weight_grads, out_returns, up_grad)
    )
    down_grad = halve_sum(after(down_part, up_grad), "context", low_bits)
    gated = (spread * gates[:, :, None]).reshape(rows, slots)
    output = middle + jnp.dot(
        gated, out_returns.reshape(slots, width).astype(F32), precision=HIGHEST
    )
    table_part = jnp.dot(diagonals[:, 0, rows:], bucket_match, precision=HIGHEST)
    table_line = lax.dynamic_update_slice(
        jnp.zeros((count * group, buckets), F32), table_part, (here * group, 0)
    )[:HEADS].reshape(1, HEADS * buckets)
    table_line = jnp.pad(table_line, ((0, 0), (0, width - HEADS * buckets)))
    small = jnp.concatenate([router_grad, gain_moe_grad[None, :], table_line], axis=0)
    small = jnp.pad(small, ((0, lanes * SPARE - small.shape[0]), (0, 0))).astype(BF16)
    chunk = 3 * held // lanes
    pack = jnp.concatenate(
        [weight_grads.reshape(lanes, chunk, width), small.reshape(lanes, SPARE, width)], axis=1
    )
    pack = halve_sum(pack, "expert", bits).astype(BF16)
    pack, down_grad = lax.optimization_barrier((pack, down_grad))
    pack = jnp.concatenate([pack, proj_rows], axis=0)
    pack = in_order(ring_parts(pack[None], "context"), "context")
    half = width // 2
    pack = jnp.concatenate(
        [
            double_gather(pack[:, :, :half], "expert", bits[:0:-1] + bits[:1], bits),
            double_gather(pack[:, :, half:], "expert", bits[1:] + bits[:1], bits),
        ],
        axis=3,
    )
    whole = jnp.moveaxis(pack[:, :, :chunk], 1, 0).reshape(count, 3, held, width)

    def rows_of(j):
        return whole[:, j].reshape(count * held, width)[:width].astype(F32)

    grad_query, grad_key, grad_value = rows_of(0).T, rows_of(1).T, rows_of(2).T
    grad_proj = pack[:, :, chunk + SPARE :].reshape(width, width).astype(F32)
    small = jnp.sum(pack[:, :, chunk : chunk + SPARE].astype(F32), axis=1).reshape(lanes * SPARE, width)
    router_total = small[:experts].T
    gain_moe_total = small[experts]
    table_total = small[experts + 1, : HEADS * buckets].reshape(HEADS, buckets).T
    gain_attn_total = (
        jnp.sum(
            grad_query * w_query.astype(F32)
            + grad_key * w_key.astype(F32)
            + grad_value * w_value.astype(F32),
            axis=1,
        )
        / gain_attn
    )

    arrived = to_context(grads_out)
    normed_grads = 0.0
    for j, weight in enumerate((w_query, w_key, w_value)):
        part = arrived[:, j].reshape(count * held, rows)[:width]
        normed_grads = normed_grads + dot(part, weight, ((0,), (1,)))
    attention_scale = lax.rsqrt(jnp.mean(source * source, axis=1, keepdims=True) + EPSILON)
    token_norm_grads, unused = normalize_back(normed_grads, source, attention_scale, gain_attn)
    token_grads = (middle_grads + token_norm_grads).astype(BF16)
    return (
        output.astype(BF16),
        token_grads,
        gain_attn_total,
        grad_query,
        grad_key,
        grad_value,
        grad_proj,
        table_total,
        gain_moe_total,
        router_total,
        up_grad[None],
        down_grad[None],
    )


def solution(mesh):
    return jax.shard_map(
        shards,
        mesh=mesh,
        in_specs=(
            P(("expert", "context"), None),
            P(),
            P(),
            P(),
            P(),
            P(),
            P(),
            P(),
            P(),
            P("expert", None, None),
            P("expert", None, None),
            P(("expert", "context"), None),
            P(),
            P(("expert", "context"), None),
        ),
        out_specs=(
            P(("expert", "context"), None),
            P(("expert", "context"), None),
            P(),
            P(),
            P(),
            P(),
            P(),
            P(),
            P(),
            P(),
            P("expert", None, "context"),
            P("expert", "context", None),
        ),
        check_vma=False,
    )
```

```python
from functools import partial

import jax
import jax.numpy as jnp
from jax import lax
from jax.experimental import pallas as pl
from jax.experimental.pallas import tpu as pltpu
from jax.sharding import PartitionSpec as P

HEADS = 12
EPSILON = 1e-06
HIGHEST = lax.Precision.HIGHEST
MASKED = -1000000000.0
F32 = jnp.float32
BF16 = jnp.bfloat16
VMEM_LIMIT = 56 * 1024 * 1024
FF_TILE = 512
SPARE = 8
ROW_TILE = 512


def dot(left, right, dims=((1,), (0,))):
    return lax.dot_general(left, right, (dims, ((), ())), preferred_element_type=F32)


def normalize(value, gain):
    scale = lax.rsqrt(jnp.mean(value * value, axis=1, keepdims=True) + EPSILON)
    return (value * scale * gain, scale)


def normalize_back(grad, value, scale, gain):
    normal = value * scale
    inner = grad * gain
    gain_grad = jnp.sum(grad * normal, axis=0)
    value_grad = scale * (inner - normal * jnp.mean(inner * normal, axis=1, keepdims=True))
    return (value_grad, gain_grad)


def shift(value, axis, step):
    count = lax.axis_size(axis)
    return lax.ppermute(value, axis, [(i, (i + step) % count) for i in range(count)])


def swap(value, axis, bit):
    count = lax.axis_size(axis)
    return lax.ppermute(value, axis, [(i, i ^ bit) for i in range(count)])


def after(value, *others):
    return lax.optimization_barrier((value, others))[0]


def ring_parts(value, axis, hold=None):
    count = lax.axis_size(axis)
    parts = [(0, value)]
    right = left = value
    for step in range(1, count // 2 + 1):
        if step == 2 and hold is not None:
            right, left = after((right, left), hold)
        right = shift(right, axis, 1)
        parts.append((step, right))
        if step <= (count - 1) // 2:
            left = shift(left, axis, -1)
            parts.append((count - step, left))
    return parts


def in_order(parts, axis):
    count = lax.axis_size(axis)
    here = lax.axis_index(axis)
    value = parts[0][1]
    size = value.shape[0]
    whole = jnp.zeros((count * size,) + value.shape[1:], value.dtype)
    for step, part in parts:
        whole = lax.dynamic_update_slice_in_dim(
            whole, part, lax.rem(here - step + count, count) * size, 0
        )
    return whole


def bit_orders(count):
    bits = [1 << i for i in range(count.bit_length() - 1)]
    return bits[:1] + bits[:0:-1]


def halve_sum(value, axis, bits, low=BF16):
    here = lax.axis_index(axis)
    for bit in bits:
        pair = value.reshape((2, value.shape[0] // 2) + value.shape[1:])
        mine = lax.rem(here // bit, 2)
        kept = lax.dynamic_index_in_dim(pair, mine, 0, keepdims=False)
        sent = lax.dynamic_index_in_dim(pair, 1 - mine, 0, keepdims=False).astype(low)
        value = kept.astype(F32) + swap(sent, axis, bit).astype(F32)
    return value[0]


def double_gather(value, axis, order):
    for bit in order:
        value = jnp.stack([value, swap(value, axis, bit)])
    return value


def attend_kernel(tokens, gain, weight, bias, normed, qkv, mixed, exact, log_total, tiles):
    length = tokens.shape[0]
    count, size, tile = mixed.shape

    @pl.when(pl.program_id(0) == 0)
    def _():
        def body(i, carry):
            part = pl.ds(i * tile, tile)
            normal, unused = normalize(tokens[part, :].astype(F32), gain[...])
            normed[part, :] = normal.astype(BF16)
            return carry

        lax.fori_loop(0, count, body, 0)

    weight_all = weight[...].reshape(3 * size, weight.shape[2])
    key_parts = []
    for i in range(count):
        part = dot(weight_all, normed[i * tile : (i + 1) * tile, :], ((1,), (1,)))
        low = part.astype(BF16)
        for j in range(3):
            qkv[j, :, i * tile : (i + 1) * tile] = low[j * size : (j + 1) * size, :]
        key_parts.append(part[size : 2 * size, :].T.astype(BF16))
        wide = jnp.broadcast_to(bias[0, :, i * tile : (i + 2) * tile], (tile, 2 * tile))
        turned = pltpu.roll(wide, tile, 1, stride=1, stride_axis=0)
        tiles[(count - 1 - i) * tile : (count - i) * tile, :] = turned[:, :tile]
    keys = jnp.concatenate(key_parts, axis=0)
    factor = size ** (-0.5)
    for i in range(count):
        cols = slice(i * tile, (i + 1) * tile)
        many = (i + 1) * tile
        scores = dot(keys[:many], qkv[0, :, cols]) * factor + tiles[length - many :, :]
        peak = jnp.max(scores, axis=0, keepdims=True)
        weights = jnp.exp(scores - peak)
        total = jnp.sum(weights, axis=0, keepdims=True)
        result = dot(qkv[2, :, :many], weights.astype(BF16)) * (1.0 / total)
        exact[0, :, cols] = result
        mixed[i, :, :] = result.astype(BF16)
        log_total[0, :, cols] = peak + jnp.log(total)


def fold(grid):
    tile = grid.shape[0]
    value = jnp.concatenate([jnp.zeros_like(grid), grid], axis=1)
    half = tile // 2
    while half >= 8:
        value = value[:half] + pltpu.roll(value[half:], 2 * tile - half, 1)
        half //= 2
    return value


def attend_back_kernel(
    qkv, normed, bias, log_total, exact, grads_in, grads, weight_grads, diagonals,
    tiles, sums, keys_acc, values_acc, query_acc,
):
    count, size, tile = grads_in.shape
    factor = size ** (-0.5)
    queries, values, outs, deltas = [], [], [], []
    keys = []
    for i in range(count):
        cols = slice(i * tile, (i + 1) * tile)
        queries.append(qkv[0, :, cols].astype(F32).T.astype(BF16))
        keys.append(qkv[1, :, cols].astype(F32).T.astype(BF16))
        values.append(qkv[2, :, cols].astype(F32).T.astype(BF16))
        out = grads_in[i].astype(F32)
        outs.append(out.T.astype(BF16))
        deltas.append(jnp.sum(out * exact[0, :, cols], axis=0, keepdims=True))
        wide = jnp.broadcast_to(bias[0, :, i * tile : (i + 2) * tile], (tile, 2 * tile))
        turned = pltpu.roll(wide, tile, 1, stride=1, stride_axis=0)
        tiles[i] = turned[:, :tile]
    for d in range(count):
        for j in range(count - d):
            i = j + d
            cols = slice(i * tile, (i + 1) * tile)
            scores = dot(keys[j], qkv[0, :, cols]) * factor + tiles[d]
            probs = jnp.exp(scores - log_total[0, :, cols])
            prob_grads = dot(values[j], grads_in[i])
            score_grads = probs * (prob_grads - deltas[i])
            low = score_grads.astype(BF16)
            value_part = dot(probs.astype(BF16), outs[i])
            key_part = dot(low, queries[i])
            query_part = dot(qkv[1, :, j * tile : (j + 1) * tile], low)
            if j == 0:
                sums[...] = score_grads
            else:
                sums[...] += score_grads
            if d == 0:
                values_acc[j] = value_part
                keys_acc[j] = key_part
                query_acc[i] = query_part
            else:
                values_acc[j] += value_part
                keys_acc[j] += key_part
                query_acc[i] += query_part
        rows = fold(sums[...])
        line = rows[0:1]
        for r in range(1, 8):
            line = line + pltpu.roll(rows[r : r + 1], 2 * tile - r, 1)
        if d == 0:
            diagonals[0, :, : 2 * tile] = line
        else:
            diagonals[0, :, d * tile : (d + 1) * tile] += line[:, :tile]
            diagonals[0, :, (d + 1) * tile : (d + 2) * tile] = line[:, tile:]
    total = None
    for i in range(count):
        query_part = (query_acc[i] * factor).astype(BF16)
        key_part = (keys_acc[i] * factor).T.astype(BF16)
        value_part = values_acc[i].T.astype(BF16)
        grads[i, 0] = query_part
        grads[i, 1] = key_part
        grads[i, 2] = value_part
        stacked = jnp.concatenate([query_part, key_part, value_part], axis=0)
        part = dot(stacked, normed[i * tile : (i + 1) * tile, :])
        total = part if total is None else total + part
    for j in range(3):
        weight_grads[j] = total[j * size : (j + 1) * size, :].astype(BF16)


def gelu_parts(hidden):
    below = 0.5 * (1.0 + lax.erf(hidden * (0.5**0.5)))
    density = jnp.exp(-0.5 * hidden * hidden) * 0.3989422804014327
    return (hidden * below).astype(BF16), below + hidden * density


def scaled_rows(target, start, gate, upstream):
    lanes, capacity = gate.shape[0], gate.shape[2]
    for i in range(lanes):
        column = jnp.broadcast_to(gate[i], (8, capacity)).T[:, :1]
        grads = column * upstream[i, :capacity, :].astype(F32)
        target[start + i * capacity : start + (i + 1) * capacity, :] = grads.astype(BF16)


def expert_kernel(rows_in, upstream, gate, up, down, outs, row_grads, out_grads, acc, sums, out_acc):
    step = pl.program_id(0)
    lanes, capacity = gate.shape[0], gate.shape[2]

    @pl.when(step == 0)
    def _():
        scaled_rows(out_grads, 0, gate, upstream)
        acc[...] = jnp.zeros_like(acc)
        out_acc[...] = jnp.zeros_like(out_acc)
        sums[...] = jnp.zeros_like(sums)

    hidden = dot(rows_in[...], up[...])
    active_grads = dot(out_grads[...], down[...], ((1,), (1,)))
    low_active, slope = gelu_parts(hidden)
    low_grads = (active_grads * slope).astype(BF16)
    out_acc[...] += dot(low_active, down[...])
    acc[...] += dot(low_grads, up[...], ((1,), (1,)))
    weighted = low_active.astype(F32) * active_grads
    part = weighted[:, :128]
    for i in range(1, weighted.shape[1] // 128):
        part = part + weighted[:, i * 128 : (i + 1) * 128]
    sums[...] += part

    @pl.when(step == pl.num_programs(0) - 1)
    def _():
        outs[...] = out_acc[...].astype(BF16)
        low = acc[...].astype(BF16)
        for i in range(lanes):
            rows = slice(i * capacity, (i + 1) * capacity)
            row_grads[i, :capacity, :] = low[rows, :]
            line = jnp.sum(sums[rows, :].T, axis=0, keepdims=True)
            high = line.astype(BF16).astype(F32)
            both = jnp.concatenate([high, line - high, jnp.zeros((SPARE - 2, capacity), F32)])
            row_grads[i, capacity:, :] = jnp.zeros((SPARE, row_grads.shape[2]), BF16)
            row_grads[i, capacity:, :capacity] = both.astype(BF16)


def expert_grads_kernel(
    index, own_rows, other_rows, own_upstream, other_upstream, own_gate, other_gate, up, down,
    up_grad, down_grad, turned, out_grads, active, hidden_grads,
):
    half = own_rows.shape[0]
    tile = min(ROW_TILE, half)

    @pl.when(pl.program_id(0) == 0)
    def _():
        scaled_rows(out_grads, 0, own_gate, own_upstream)
        scaled_rows(out_grads, half, other_gate, other_upstream)
        for start in range(0, half, tile):
            rows = slice(start, start + tile)
            turned[:, rows] = own_rows[rows, :].T
            turned[:, half + start : half + start + tile] = other_rows[rows, :].T

    for base, source in ((0, own_rows), (half, other_rows)):
        for start in range(0, half, tile):
            rows = slice(base + start, base + start + tile)
            hidden = dot(source[start : start + tile, :], up[...])
            active_grads = dot(out_grads[rows, :], down[...], ((1,), (1,)))
            low_active, slope = gelu_parts(hidden)
            active[rows, :] = low_active
            hidden_grads[rows, :] = (active_grads * slope).astype(BF16)
    up_grad[0] = dot(turned[...], hidden_grads[...]).astype(BF16)
    down_grad[0] = dot(active[...], out_grads[...], ((0,), (0,))).astype(BF16)


def params():
    return pltpu.CompilerParams(
        dimension_semantics=("arbitrary",), vmem_limit_bytes=VMEM_LIMIT
    )


def cost(flops, size):
    return pl.CostEstimate(flops=flops, bytes_accessed=size, transcendentals=0)


def attend(tokens, gain, weight, bias, count):
    length, width = tokens.shape
    group = bias.shape[0]
    size = weight.shape[1] // group
    tile = length // count
    return pl.pallas_call(
        attend_kernel,
        grid=(group,),
        in_specs=[
            pl.BlockSpec((length, width), lambda h: (0, 0)),
            pl.BlockSpec((1, width), lambda h: (0, 0)),
            pl.BlockSpec((3, size, width), lambda h: (0, h, 0)),
            pl.BlockSpec((1, 1, length + tile), lambda h: (h, 0, 0)),
        ],
        out_specs=[
            pl.BlockSpec((length, width), lambda h: (0, 0)),
            pl.BlockSpec((3, size, length), lambda h: (0, h, 0)),
            pl.BlockSpec((count, size, tile), lambda h: (0, h, 0)),
            pl.BlockSpec((1, size, length), lambda h: (h, 0, 0)),
            pl.BlockSpec((1, 1, length), lambda h: (h, 0, 0)),
        ],
        out_shape=[
            jax.ShapeDtypeStruct((length, width), BF16),
            jax.ShapeDtypeStruct((3, group * size, length), BF16),
            jax.ShapeDtypeStruct((count, group * size, tile), BF16),
            jax.ShapeDtypeStruct((group, size, length), F32),
            jax.ShapeDtypeStruct((group, 1, length), F32),
        ],
        scratch_shapes=[pltpu.VMEM((length, tile), F32)],
        compiler_params=params(),
        cost_estimate=cost(14 * length * width * size * group, 8 * length * width),
        name="attend",
    )(tokens, gain, weight, bias)


def attend_back(qkv, normed, bias, log_total, exact, grads_in):
    length, width = normed.shape
    count, _, tile = grads_in.shape
    group, size, _ = exact.shape
    return pl.pallas_call(
        attend_back_kernel,
        grid=(group,),
        in_specs=[
            pl.BlockSpec((3, size, length), lambda h: (0, h, 0)),
            pl.BlockSpec((length, width), lambda h: (0, 0)),
            pl.BlockSpec((1, 1, length + tile), lambda h: (h, 0, 0)),
            pl.BlockSpec((1, 1, length), lambda h: (h, 0, 0)),
            pl.BlockSpec((1, size, length), lambda h: (h, 0, 0)),
            pl.BlockSpec((count, size, tile), lambda h: (0, h, 0)),
        ],
        out_specs=[
            pl.BlockSpec((count, 3, size, tile), lambda h: (0, 0, h, 0)),
            pl.BlockSpec((3, size, width), lambda h: (0, h, 0)),
            pl.BlockSpec((1, 1, length + tile), lambda h: (h, 0, 0)),
        ],
        out_shape=[
            jax.ShapeDtypeStruct((count, 3, group * size, tile), BF16),
            jax.ShapeDtypeStruct((3, group * size, width), BF16),
            jax.ShapeDtypeStruct((group, 1, length + tile), F32),
        ],
        scratch_shapes=[
            pltpu.VMEM((count, tile, tile), F32),
            pltpu.VMEM((tile, tile), F32),
            pltpu.VMEM((count, tile, size), F32),
            pltpu.VMEM((count, tile, size), F32),
            pltpu.VMEM((count, size, tile), F32),
        ],
        compiler_params=params(),
        cost_estimate=cost(18 * length * width * size * group, 8 * length * width),
        name="attend_back",
    )(qkv, normed, bias, log_total, exact, grads_in)


def expert(rows_in, upstream, gate, up, down):
    rows, width = rows_in.shape
    hidden = up.shape[1]
    lanes, _, capacity = gate.shape
    return pl.pallas_call(
        expert_kernel,
        grid=(hidden // FF_TILE,),
        in_specs=[
            pl.BlockSpec((rows, width), lambda f: (0, 0)),
            pl.BlockSpec(upstream.shape, lambda f: (0, 0, 0)),
            pl.BlockSpec(gate.shape, lambda f: (0, 0, 0)),
            pl.BlockSpec((width, FF_TILE), lambda f: (0, f)),
            pl.BlockSpec((FF_TILE, width), lambda f: (f, 0)),
        ],
        out_specs=[
            pl.BlockSpec((rows, width), lambda f: (0, 0)),
            pl.BlockSpec((lanes, capacity + SPARE, width), lambda f: (0, 0, 0)),
        ],
        out_shape=[
            jax.ShapeDtypeStruct((rows, width), BF16),
            jax.ShapeDtypeStruct((lanes, capacity + SPARE, width), BF16),
        ],
        scratch_shapes=[
            pltpu.VMEM((rows, width), BF16),
            pltpu.VMEM((rows, width), F32),
            pltpu.VMEM((rows, 128), F32),
            pltpu.VMEM((rows, width), F32),
        ],
        compiler_params=params(),
        cost_estimate=cost(10 * rows * width * hidden, 4 * width * hidden),
        name="expert",
    )(rows_in, upstream, gate, up, down)


def expert_grads(index, own_rows, other_rows, own_upstream, other_upstream, own_gate, other_gate, up, down, count, steps):
    half, width = own_rows.shape
    hidden = up.shape[1]
    share = hidden // count
    whole = pl.BlockSpec((half, width), lambda s, i: (0, 0))
    slots = pl.BlockSpec(own_upstream.shape, lambda s, i: (0, 0, 0))
    gates = pl.BlockSpec(own_gate.shape, lambda s, i: (0, 0, 0))
    return pl.pallas_call(
        expert_grads_kernel,
        grid_spec=pltpu.PrefetchScalarGridSpec(
            num_scalar_prefetch=1,
            grid=(steps,),
            in_specs=[
                whole,
                whole,
                slots,
                slots,
                gates,
                gates,
                pl.BlockSpec((width, share), lambda s, i: (0, i[0] + s)),
                pl.BlockSpec((share, width), lambda s, i: (i[0] + s, 0)),
            ],
            out_specs=[
                pl.BlockSpec((1, width, share), lambda s, i: (s, 0, 0)),
                pl.BlockSpec((1, share, width), lambda s, i: (s, 0, 0)),
            ],
            scratch_shapes=[
                pltpu.VMEM((width, 2 * half), BF16),
                pltpu.VMEM((2 * half, width), BF16),
                pltpu.VMEM((2 * half, share), BF16),
                pltpu.VMEM((2 * half, share), BF16),
            ],
        ),
        out_shape=[
            jax.ShapeDtypeStruct((steps, width, share), BF16),
            jax.ShapeDtypeStruct((steps, share, width), BF16),
        ],
        compiler_params=params(),
        cost_estimate=cost(16 * half * width * share * steps, 8 * half * width),
        name="expert_grads",
    )(index, own_rows, other_rows, own_upstream, other_upstream, own_gate, other_gate, up, down)


def assemble_kernel(
    bits, chunk, index, near, far, query, key, value,
    query_grad, key_grad, value_grad, proj_grad, small_sum, gain_sum,
):
    outer = bits[1:]
    lanes = 1 << len(bits)
    count, depth, half = near.shape[-3:]
    own = index[0]
    first = pl.program_id(0) == 0

    def block(lane, z):
        turn = own ^ lane
        steps = [lax.rem(turn // bit, 2) for bit in outer]
        places = [jnp.where(first, a, b) for a, b in zip(steps, steps[::-1])]
        side = lax.rem(turn // bits[0], 2) == 0
        at = (0, *places, z)
        return jnp.where(side, near[at], far[at]).astype(F32)

    order = []
    for i in range(lanes):
        lane = 0
        for j, bit in enumerate(bits):
            lane += bit * ((i >> (len(bits) - 1 - j)) & 1)
        order.append(lane)
    blocks = [[block(lane, z) for z in range(count)] for lane in order]
    part = chunk // 3
    share = depth - chunk - SPARE
    for i in range(lanes):
        total = blocks[i][0][chunk : chunk + SPARE]
        for z in range(1, count):
            total = total + blocks[i][z][chunk : chunk + SPARE]
        small_sum[i * SPARE : (i + 1) * SPARE, :] = total
    proj_grad[...] = jnp.concatenate(
        [blocks[i][z][chunk + SPARE :] for i in range(lanes) for z in range(count)], axis=0
    )
    total = None
    for j, (weight, grad) in enumerate(
        ((query, query_grad), (key, key_grad), (value, value_grad))
    ):
        rows = [
            blocks[i][z][j * part : (j + 1) * part] for z in range(count) for i in range(lanes)
        ]
        whole = jnp.concatenate(rows, axis=0)[: grad.shape[1]].T
        grad[...] = whole
        sums = jnp.sum(whole * weight[...].astype(F32), axis=1, keepdims=True)
        total = sums if total is None else total + sums
    gain_sum[...] = total


def assemble(index, near, far, query, key, value, bits, chunk):
    shape = near.shape
    half = shape[-1]
    width = query.shape[0]
    lanes = 1 << len(bits)
    rows = pl.BlockSpec((half, width), lambda s, i: (s, 0))
    cols = pl.BlockSpec((width, half), lambda s, i: (0, s))
    pack = pl.BlockSpec((1,) + shape[1:], lambda s, i: (s,) + (0,) * (len(shape) - 1))
    return pl.pallas_call(
        partial(assemble_kernel, bits, chunk),
        grid_spec=pltpu.PrefetchScalarGridSpec(
            num_scalar_prefetch=1,
            grid=(shape[0],),
            in_specs=[pack, pack, rows, rows, rows],
            out_specs=[
                rows,
                rows,
                rows,
                cols,
                pl.BlockSpec((lanes * SPARE, half), lambda s, i: (0, s)),
                pl.BlockSpec((half, 1), lambda s, i: (s, 0)),
            ],
        ),
        out_shape=[jax.ShapeDtypeStruct((width, width), F32)] * 4
        + [
            jax.ShapeDtypeStruct((lanes * SPARE, width), F32),
            jax.ShapeDtypeStruct((width, 1), F32),
        ],
        compiler_params=params(),
        name="assemble",
    )(index, near, far, query, key, value)


def token_back_kernel(
    returns, dispatch, gates, chosen, middle, cotangent, gain, routed, router, proj,
    middle_grads, branch_grads, mixed_grads, gain_grad, router_grad,
):
    experts, depth, width = returns.shape
    capacity = depth - SPARE
    grads = None
    columns = []
    for i in range(experts):
        select = dispatch[:, i * capacity : (i + 1) * capacity]
        part = dot(select, returns[i, :capacity, :])
        grads = part if grads is None else grads + part
        lines = returns[i, capacity:, :].astype(F32)
        line = (lines[0:1] + lines[1:2])[:, :capacity]
        columns.append(jnp.sum(select.astype(F32) * line, axis=1, keepdims=True))
    total = columns[0]
    for column in columns[1:]:
        total = total + column
    logit_grads = []
    for i in range(experts):
        grad = (columns[i] - gates[:, i : i + 1] * total) * chosen[:, i : i + 1]
        logit_grads.append(grad)
        grads = grads + grad * router[i : i + 1, :]
        router_grad[i : i + 1, :] = jnp.sum(grad * routed[...].astype(F32), axis=0, keepdims=True)
    value = middle[...]
    scale = lax.rsqrt(jnp.mean(value * value, axis=1, keepdims=True) + EPSILON)
    normal = value * scale
    gain_grad[...] = jnp.sum(grads * normal, axis=0, keepdims=True)
    inner = grads * gain[...]
    back = scale * (inner - normal * jnp.mean(inner * normal, axis=1, keepdims=True))
    result = cotangent[...].astype(F32) + back
    middle_grads[...] = result
    low = result.astype(BF16)
    branch_grads[...] = low
    mixed_grads[...] = dot(proj[...], low, ((1,), (1,))).astype(BF16)


def token_back(returns, dispatch, gates, chosen, middle, cotangent, gain, routed, router, proj):
    rows, width = middle.shape
    return pl.pallas_call(
        token_back_kernel,
        out_shape=[
            jax.ShapeDtypeStruct((rows, width), F32),
            jax.ShapeDtypeStruct((rows, width), BF16),
            jax.ShapeDtypeStruct((width, rows), BF16),
            jax.ShapeDtypeStruct((1, width), F32),
            jax.ShapeDtypeStruct(router.shape, F32),
        ],
        compiler_params=pltpu.CompilerParams(vmem_limit_bytes=VMEM_LIMIT),
        name="token_back",
    )(returns, dispatch, gates, chosen, middle, cotangent, gain, routed, router, proj)


def chosen_softmax(logits, chosen, axis):
    peak = jnp.max(jnp.where(chosen, logits, -jnp.inf), axis=axis, keepdims=True)
    peak = jnp.where(peak > -jnp.inf, peak, 0.0)
    parts = jnp.where(chosen, jnp.exp(jnp.where(chosen, logits, peak) - peak), 0.0)
    total = jnp.sum(parts, axis=axis, keepdims=True)
    return parts / jnp.where(total > 0.0, total, 1.0)


def to_experts(value):
    return exchange(value, "expert")


def to_context(value):
    return exchange(value, "context")


def exchange(value, axis):
    return lax.all_to_all(value, axis, split_axis=0, concat_axis=0)


def exchange_steps(value, axis, send):
    count = lax.axis_size(axis)
    here = lax.axis_index(axis)
    whole = jnp.zeros_like(value)
    for step in sorted(range(count), key=lambda k: (k != 0, -min(k, count - k))):
        target, source, part = send(here, step)
        piece = lax.dynamic_slice_in_dim(value, target, 1, 0)
        whole = lax.dynamic_update_slice_in_dim(whole, part(piece) if step else piece, source, 0)
    return whole


def expert_steps(value):
    def send(here, step):
        return here ^ step, here ^ step, lambda piece: swap(piece, "expert", step)

    return exchange_steps(value, "expert", send)


def context_steps(value, arrivals=None):
    count = lax.axis_size("context")

    def send(here, step):
        target, source = lax.rem(here + step, count), lax.rem(here - step + count, count)

        def part(piece):
            piece = shift(piece, "context", step)
            if arrivals is not None:
                arrivals.append(piece)
            return piece

        return target, source, part

    return exchange_steps(value, "context", send)


def shards(
    tokens,
    gain_attn,
    w_query,
    w_key,
    w_value,
    w_proj,
    bias_table,
    gain_moe,
    w_router,
    w_up,
    w_down,
    routes,
    bucket_ids,
    cotangent,
):
    rows, width = tokens.shape
    size = width // HEADS
    experts = w_router.shape[1]
    buckets = bias_table.shape[0]
    picks = routes.shape[1]
    capacity = 2 * rows * picks // experts
    slots = experts * capacity
    count = lax.axis_size("context")
    lanes = lax.axis_size("expert")
    here = lax.axis_index("context")
    own = lax.axis_index("expert")
    length = rows * count
    group = -(-HEADS // count)
    held = group * size
    extra = count * group - HEADS

    token_parts = ring_parts(tokens, "context")

    expert_ids = jnp.arange(experts, dtype=jnp.int32)
    order = jnp.arange(rows, dtype=jnp.int32)
    earlier = (order[:, None] > order[None, :]).astype(BF16)

    def routing(block):
        chosen = jnp.any(block[:, :, None] == expert_ids[None, None, :], axis=1)
        member = chosen.astype(BF16)
        place = dot(earlier, member).astype(jnp.int32)
        dispatch = (
            (place[:, :, None] == jnp.arange(capacity, dtype=jnp.int32)[None, None, :])
            & chosen[:, :, None]
        ).astype(BF16)
        return chosen, member, dispatch.reshape(rows, slots)

    chosen, member, dispatch = routing(routes)

    def slots_of(dispatch, block):
        sent = dot(dispatch, block, ((0,), (0,))).astype(BF16)
        return sent.reshape(experts, capacity, width)

    def upstream_sent(member, dispatch, block):
        choices = dot(member, dispatch, ((0,), (0,))).astype(BF16)
        choices = jnp.transpose(choices.reshape(experts, experts, capacity), (1, 0, 2))
        choices = jnp.pad(choices, ((0, 0), (0, 0), (0, width - capacity)))
        return jnp.concatenate([slots_of(dispatch, block), choices], axis=1)

    partner = count // 2

    def head_rows(weight):
        whole = jnp.pad(weight, ((0, 0), (0, extra * size)))
        return lax.dynamic_slice_in_dim(whole, here * held, held, 1).T

    head_weights = jnp.stack([head_rows(w) for w in (w_query, w_key, w_value)])

    own_sent, head_weights = after(
        (upstream_sent(member, dispatch, cotangent), head_weights), token_parts[2][1]
    )
    upstream_slots = to_experts(own_sent)
    sequence = in_order(token_parts, "context")
    cotangent_other, routes_other = after((cotangent, routes.T), sequence)
    cotangent_other = swap(cotangent_other, "context", partner)
    routes_other = swap(routes_other, "context", partner)

    bucket_match = (
        bucket_ids[:, None] == jnp.arange(buckets, dtype=jnp.int32)[None, :]
    ).astype(F32)
    per_distance = lax.dot_general(
        jnp.pad(bias_table, ((0, 0), (0, extra))), bucket_match, (((0,), (1,)), ((), ())),
        precision=HIGHEST,
    )
    bias = jnp.pad(
        lax.dynamic_slice_in_dim(per_distance, here * group, group, 0),
        ((0, 0), (rows, 0)),
        constant_values=MASKED,
    )[:, None, :]
    normed, qkv, mixed_parts, exact, log_total = attend(
        sequence, gain_attn[None, :], head_weights, bias, count
    )
    mixed_parts, upstream_slots, cotangent_other, routes_other = lax.optimization_barrier(
        (mixed_parts, upstream_slots, cotangent_other, routes_other)
    )
    unused, member_other, dispatch_other = routing(routes_other.T)
    upstream_other = to_experts(upstream_sent(member_other, dispatch_other, cotangent_other))
    mixed = context_steps(mixed_parts).reshape(count * held, rows)[:width]
    source = tokens.astype(F32)
    middle = source + dot(mixed, w_proj, ((0,), (0,)))
    moe_normal, moe_scale = normalize(middle, gain_moe)
    routed = moe_normal.astype(BF16)

    logits = dot(routed, w_router)
    gates = chosen_softmax(logits, chosen, 1)

    def gates_of(received, upstream):
        choices = jnp.moveaxis(upstream[:, capacity:, :capacity], 1, 0) > 0.5
        slot_logits = dot(w_router, received, ((0,), (1,))).reshape(experts, lanes, capacity)
        slot_gates = chosen_softmax(slot_logits, choices, 0)
        return lax.dynamic_index_in_dim(slot_gates, own, 0, keepdims=False)[:, None, :]

    sent, upstream_other = lax.optimization_barrier((slots_of(dispatch, routed), upstream_other))
    received = to_experts(sent).reshape(slots, width)
    routed_other = swap(routed, "context", partner)
    received, routed_other = lax.optimization_barrier((received, routed_other))
    received_other = to_experts(slots_of(dispatch_other, routed_other)).reshape(slots, width)
    slot_gate = gates_of(received, upstream_slots)
    expert_out, row_grads = expert(received, upstream_slots, slot_gate, w_up[0], w_down[0])
    row_grads, received_other = lax.optimization_barrier((row_grads, received_other))
    row_returns = to_experts(row_grads)

    quarter = partner // 2
    mine = lax.rem(here // quarter, 2)
    first = (here // partner) * partner
    other_gate = gates_of(received_other, upstream_other)

    def gradients(start, hold):
        return expert_grads(
            after(start, hold)[None],
            received,
            received_other,
            upstream_slots,
            upstream_other,
            slot_gate,
            other_gate,
            w_up[0],
            w_down[0],
            count,
            quarter,
        )

    up_sent, down_sent = gradients(first + (1 - mine) * quarter, row_grads)
    up_kept, down_kept = gradients(first + mine * quarter, down_sent)
    row_returns, down_sent, up_kept, down_kept = lax.optimization_barrier(
        (row_returns, down_sent, up_kept, down_kept)
    )
    up_arrived = swap(up_sent, "context", quarter)
    low_bits = [1 << i for i in range(quarter.bit_length() - 1)][::-1]
    spread = dispatch.reshape(rows, experts, capacity).astype(F32)
    middle_grads, branch_grads, mixed_grads, gain_moe_grad, router_grad = token_back(
        row_returns,
        dispatch,
        gates,
        chosen.astype(F32),
        middle,
        cotangent,
        gain_moe[None, :],
        routed,
        w_router.astype(F32).T,
        w_proj,
    )
    arrivals = []
    grads_in = context_steps(
        jnp.pad(mixed_grads, ((0, extra * size), (0, 0))).reshape(count, held, rows),
        arrivals,
    )
    bits = bit_orders(lanes)
    out_returns = to_experts(after(expert_out, arrivals[0]).reshape(experts, capacity, width))
    grads_in, up_arrived = lax.optimization_barrier((grads_in, up_arrived))
    proj_part = dot(mixed, branch_grads).astype(BF16).reshape(lanes, width // lanes, width)
    proj_part = halve_sum(proj_part, "expert", bits).astype(BF16)
    proj_part = context_steps(proj_part.reshape(count, width // (lanes * count), width))
    proj_rows = jnp.sum(proj_part.astype(F32), axis=0).astype(BF16)

    grads_out, weight_grads, diagonals = attend_back(
        qkv, normed, bias, log_total, exact, grads_in
    )
    weight_grads, out_returns = lax.optimization_barrier((weight_grads, out_returns))
    cut = down_sent.shape[1] // 2
    down_first = swap(after(down_sent[:, :cut], up_arrived), "context", quarter)
    weight_grads, down_first = lax.optimization_barrier((weight_grads, down_first))
    table_part = jnp.dot(diagonals[:, 0, rows:], bucket_match, precision=HIGHEST)
    table_line = lax.dynamic_update_slice(
        jnp.zeros((count * group, buckets), F32), table_part, (here * group, 0)
    )[:HEADS].reshape(1, HEADS * buckets)
    table_line = jnp.pad(table_line, ((0, 0), (0, width - HEADS * buckets)))
    small = jnp.concatenate([router_grad, gain_moe_grad, table_line], axis=0)
    small = jnp.pad(small, ((0, lanes * SPARE - small.shape[0]), (0, 0))).astype(BF16)
    chunk = 3 * held // lanes
    pack = jnp.concatenate(
        [
            jnp.moveaxis(weight_grads.reshape(3, lanes, held // lanes, width), 1, 0).reshape(
                lanes, chunk, width
            ),
            small.reshape(lanes, SPARE, width),
        ],
        axis=1,
    )
    pack = halve_sum(pack, "expert", bits).astype(BF16)
    pack = jnp.concatenate([pack, proj_rows], axis=0)
    pack = in_order(ring_parts(pack[None], "context"), "context")
    down_second, grads_out = after((down_sent[:, cut:], grads_out), pack)
    down_second = swap(down_second, "context", quarter)
    arrived = context_steps(grads_out)
    up_grad = up_kept.astype(F32) + up_arrived.astype(F32)
    gated = (spread * gates[:, :, None]).reshape(rows, slots)
    output = middle + jnp.dot(
        gated, out_returns.reshape(slots, width).astype(F32), precision=HIGHEST
    )
    half = width // 2
    near = jnp.stack(
        [
            double_gather(pack[:, :, :half], "expert", bits[:0:-1]),
            double_gather(pack[:, :, half:], "expert", bits[1:]),
        ]
    )
    near, arrived, down_second = lax.optimization_barrier((near, arrived, down_second))
    far = swap(near, "expert", bits[0])
    down_arrived = jnp.concatenate([down_first, down_second], axis=1)
    down_grad = down_kept.astype(F32) + down_arrived.astype(F32)
    up_grad = halve_sum(up_grad, "context", low_bits, BF16)
    down_grad = halve_sum(down_grad, "context", low_bits, BF16)
    grad_query, grad_key, grad_value, grad_proj, small, gain_attn_total = assemble(
        own[None], near, far, w_query, w_key, w_value, bits, chunk
    )
    gain_attn_total = gain_attn_total[:, 0] / gain_attn
    router_total = small[:experts].T
    gain_moe_total = small[experts]
    table_total = small[experts + 1, : HEADS * buckets].reshape(HEADS, buckets).T
    normed_grads = 0.0
    for j, weight in enumerate((w_query, w_key, w_value)):
        part = arrived[:, j].reshape(count * held, rows)[:width]
        normed_grads = normed_grads + dot(part, weight, ((0,), (1,)))
    attention_scale = lax.rsqrt(jnp.mean(source * source, axis=1, keepdims=True) + EPSILON)
    token_norm_grads, unused = normalize_back(normed_grads, source, attention_scale, gain_attn)
    token_grads = (middle_grads + token_norm_grads).astype(BF16)
    return (
        output.astype(BF16),
        token_grads,
        gain_attn_total,
        grad_query,
        grad_key,
        grad_value,
        grad_proj,
        table_total,
        gain_moe_total,
        router_total,
        up_grad[None],
        down_grad[None],
    )


def solution(mesh):
    return jax.shard_map(
        shards,
        mesh=mesh,
        in_specs=(
            P(("expert", "context"), None),
            P(),
            P(),
            P(),
            P(),
            P(),
            P(),
            P(),
            P(),
            P("expert", None, None),
            P("expert", None, None),
            P(("expert", "context"), None),
            P(),
            P(("expert", "context"), None),
        ),
        out_specs=(
            P(("expert", "context"), None),
            P(("expert", "context"), None),
            P(),
            P(),
            P(),
            P(),
            P(),
            P(),
            P(),
            P(),
            P("expert", None, "context"),
            P("expert", "context", None),
        ),
        check_vma=False,
    )
```

```python
from functools import partial

import jax
import jax.numpy as jnp
from jax import lax
from jax.experimental import pallas as pl
from jax.experimental.pallas import tpu as pltpu
from jax.sharding import PartitionSpec as P

HEADS = 12
EPSILON = 1e-06
HIGHEST = lax.Precision.HIGHEST
MASKED = -1000000000.0
F32 = jnp.float32
BF16 = jnp.bfloat16
VMEM_LIMIT = 56 * 1024 * 1024
FF_TILE = 512
SPARE = 8
ROW_TILE = 512


def dot(left, right, dims=((1,), (0,))):
    return lax.dot_general(left, right, (dims, ((), ())), preferred_element_type=F32)


def normalize(value, gain):
    scale = lax.rsqrt(jnp.mean(value * value, axis=1, keepdims=True) + EPSILON)
    return (value * scale * gain, scale)


def normalize_back(grad, value, scale, gain):
    normal = value * scale
    inner = grad * gain
    gain_grad = jnp.sum(grad * normal, axis=0)
    value_grad = scale * (inner - normal * jnp.mean(inner * normal, axis=1, keepdims=True))
    return (value_grad, gain_grad)


def shift(value, axis, step):
    count = lax.axis_size(axis)
    return lax.ppermute(value, axis, [(i, (i + step) % count) for i in range(count)])


def swap(value, axis, bit):
    count = lax.axis_size(axis)
    return lax.ppermute(value, axis, [(i, i ^ bit) for i in range(count)])


def after(value, *others):
    return lax.optimization_barrier((value, others))[0]


def ring_parts(value, axis, hold=None):
    count = lax.axis_size(axis)
    parts = [(0, value)]
    right = left = value
    for step in range(1, count // 2 + 1):
        if step == 2 and hold is not None:
            right, left = after((right, left), hold)
        right = shift(right, axis, 1)
        parts.append((step, right))
        if step <= (count - 1) // 2:
            left = shift(left, axis, -1)
            parts.append((count - step, left))
    return parts


def in_order(parts, axis):
    count = lax.axis_size(axis)
    here = lax.axis_index(axis)
    value = parts[0][1]
    size = value.shape[0]
    whole = jnp.zeros((count * size,) + value.shape[1:], value.dtype)
    for step, part in parts:
        whole = lax.dynamic_update_slice_in_dim(
            whole, part, lax.rem(here - step + count, count) * size, 0
        )
    return whole


def bit_orders(count):
    bits = [1 << i for i in range(count.bit_length() - 1)]
    return bits[:1] + bits[:0:-1]


def halve_sum(value, axis, bits, low=BF16):
    here = lax.axis_index(axis)
    for bit in bits:
        pair = value.reshape((2, value.shape[0] // 2) + value.shape[1:])
        mine = lax.rem(here // bit, 2)
        kept = lax.dynamic_index_in_dim(pair, mine, 0, keepdims=False)
        sent = lax.dynamic_index_in_dim(pair, 1 - mine, 0, keepdims=False).astype(low)
        value = kept.astype(F32) + swap(sent, axis, bit).astype(F32)
    return value[0]


def double_gather(value, axis, order):
    for bit in order:
        value = jnp.stack([value, swap(value, axis, bit)])
    return value


def attend_kernel(tokens, gain, weight, bias, normed, qkv, mixed, exact, log_total, tiles):
    length = tokens.shape[0]
    count, size, tile = mixed.shape

    @pl.when(pl.program_id(0) == 0)
    def _():
        def body(i, carry):
            part = pl.ds(i * tile, tile)
            normal, unused = normalize(tokens[part, :].astype(F32), gain[...])
            normed[part, :] = normal.astype(BF16)
            return carry

        lax.fori_loop(0, count, body, 0)

    weight_all = weight[...].reshape(3 * size, weight.shape[2])
    key_parts = []
    for i in range(count):
        part = dot(weight_all, normed[i * tile : (i + 1) * tile, :], ((1,), (1,)))
        low = part.astype(BF16)
        for j in range(3):
            qkv[j, :, i * tile : (i + 1) * tile] = low[j * size : (j + 1) * size, :]
        key_parts.append(part[size : 2 * size, :].T.astype(BF16))
        wide = jnp.broadcast_to(bias[0, :, i * tile : (i + 2) * tile], (tile, 2 * tile))
        turned = pltpu.roll(wide, tile, 1, stride=1, stride_axis=0)
        tiles[(count - 1 - i) * tile : (count - i) * tile, :] = turned[:, :tile]
    keys = jnp.concatenate(key_parts, axis=0)
    factor = size ** (-0.5)
    for i in range(count):
        cols = slice(i * tile, (i + 1) * tile)
        many = (i + 1) * tile
        scores = dot(keys[:many], qkv[0, :, cols]) * factor + tiles[length - many :, :]
        peak = jnp.max(scores, axis=0, keepdims=True)
        weights = jnp.exp(scores - peak)
        total = jnp.sum(weights, axis=0, keepdims=True)
        result = dot(qkv[2, :, :many], weights.astype(BF16)) * (1.0 / total)
        exact[0, :, cols] = result
        mixed[i, :, :] = result.astype(BF16)
        log_total[0, :, cols] = peak + jnp.log(total)


def fold(grid):
    tile = grid.shape[0]
    value = jnp.concatenate([jnp.zeros_like(grid), grid], axis=1)
    half = tile // 2
    while half >= 8:
        value = value[:half] + pltpu.roll(value[half:], 2 * tile - half, 1)
        half //= 2
    return value


def attend_back_kernel(
    qkv, normed, bias, log_total, exact, grads_in, grads, weight_grads, diagonals,
    tiles, sums, keys_acc, values_acc, query_acc,
):
    count, size, tile = grads_in.shape
    factor = size ** (-0.5)
    queries, values, outs, deltas = [], [], [], []
    keys = []
    for i in range(count):
        cols = slice(i * tile, (i + 1) * tile)
        queries.append(qkv[0, :, cols].astype(F32).T.astype(BF16))
        keys.append(qkv[1, :, cols].astype(F32).T.astype(BF16))
        values.append(qkv[2, :, cols].astype(F32).T.astype(BF16))
        out = grads_in[i].astype(F32)
        outs.append(out.T.astype(BF16))
        deltas.append(jnp.sum(out * exact[0, :, cols], axis=0, keepdims=True))
        wide = jnp.broadcast_to(bias[0, :, i * tile : (i + 2) * tile], (tile, 2 * tile))
        turned = pltpu.roll(wide, tile, 1, stride=1, stride_axis=0)
        tiles[i] = turned[:, :tile]
    for d in range(count):
        for j in range(count - d):
            i = j + d
            cols = slice(i * tile, (i + 1) * tile)
            scores = dot(keys[j], qkv[0, :, cols]) * factor + tiles[d]
            probs = jnp.exp(scores - log_total[0, :, cols])
            prob_grads = dot(values[j], grads_in[i])
            score_grads = probs * (prob_grads - deltas[i])
            low = score_grads.astype(BF16)
            value_part = dot(probs.astype(BF16), outs[i])
            key_part = dot(low, queries[i])
            query_part = dot(qkv[1, :, j * tile : (j + 1) * tile], low)
            if j == 0:
                sums[...] = score_grads
            else:
                sums[...] += score_grads
            if d == 0:
                values_acc[j] = value_part
                keys_acc[j] = key_part
                query_acc[i] = query_part
            else:
                values_acc[j] += value_part
                keys_acc[j] += key_part
                query_acc[i] += query_part
        rows = fold(sums[...])
        line = rows[0:1]
        for r in range(1, 8):
            line = line + pltpu.roll(rows[r : r + 1], 2 * tile - r, 1)
        if d == 0:
            diagonals[0, :, : 2 * tile] = line
        else:
            diagonals[0, :, d * tile : (d + 1) * tile] += line[:, :tile]
            diagonals[0, :, (d + 1) * tile : (d + 2) * tile] = line[:, tile:]
    total = None
    for i in range(count):
        query_part = (query_acc[i] * factor).astype(BF16)
        key_part = (keys_acc[i] * factor).T.astype(BF16)
        value_part = values_acc[i].T.astype(BF16)
        grads[i, 0] = query_part
        grads[i, 1] = key_part
        grads[i, 2] = value_part
        stacked = jnp.concatenate([query_part, key_part, value_part], axis=0)
        part = dot(stacked, normed[i * tile : (i + 1) * tile, :])
        total = part if total is None else total + part
    for j in range(3):
        weight_grads[j] = total[j * size : (j + 1) * size, :].astype(BF16)


def gelu_parts(hidden):
    below = 0.5 * (1.0 + lax.erf(hidden * (0.5**0.5)))
    density = jnp.exp(-0.5 * hidden * hidden) * 0.3989422804014327
    return (hidden * below).astype(BF16), below + hidden * density


def scaled_rows(target, start, gate, upstream):
    lanes, capacity = gate.shape[0], gate.shape[2]
    for i in range(lanes):
        column = jnp.broadcast_to(gate[i], (8, capacity)).T[:, :1]
        grads = column * upstream[i, :capacity, :].astype(F32)
        target[start + i * capacity : start + (i + 1) * capacity, :] = grads.astype(BF16)


def expert_kernel(rows_in, upstream, gate, up, down, outs, row_grads, out_grads, acc, sums, out_acc):
    step = pl.program_id(0)
    lanes, capacity = gate.shape[0], gate.shape[2]

    @pl.when(step == 0)
    def _():
        scaled_rows(out_grads, 0, gate, upstream)
        acc[...] = jnp.zeros_like(acc)
        out_acc[...] = jnp.zeros_like(out_acc)
        sums[...] = jnp.zeros_like(sums)

    hidden = dot(rows_in[...], up[...])
    active_grads = dot(out_grads[...], down[...], ((1,), (1,)))
    low_active, slope = gelu_parts(hidden)
    low_grads = (active_grads * slope).astype(BF16)
    out_acc[...] += dot(low_active, down[...])
    acc[...] += dot(low_grads, up[...], ((1,), (1,)))
    weighted = low_active.astype(F32) * active_grads
    part = weighted[:, :128]
    for i in range(1, weighted.shape[1] // 128):
        part = part + weighted[:, i * 128 : (i + 1) * 128]
    sums[...] += part

    @pl.when(step == pl.num_programs(0) - 1)
    def _():
        outs[...] = out_acc[...].astype(BF16)
        low = acc[...].astype(BF16)
        for i in range(lanes):
            rows = slice(i * capacity, (i + 1) * capacity)
            row_grads[i, :capacity, :] = low[rows, :]
            line = jnp.sum(sums[rows, :].T, axis=0, keepdims=True)
            high = line.astype(BF16).astype(F32)
            both = jnp.concatenate([high, line - high, jnp.zeros((SPARE - 2, capacity), F32)])
            row_grads[i, capacity:, :] = jnp.zeros((SPARE, row_grads.shape[2]), BF16)
            row_grads[i, capacity:, :capacity] = both.astype(BF16)


def expert_grads_kernel(
    index, own_rows, other_rows, own_upstream, other_upstream, own_gate, other_gate, up, down,
    up_grad, down_grad, turned, out_grads, active, hidden_grads,
):
    half = own_rows.shape[0]
    tile = min(ROW_TILE, half)

    @pl.when(pl.program_id(0) == 0)
    def _():
        scaled_rows(out_grads, 0, own_gate, own_upstream)
        scaled_rows(out_grads, half, other_gate, other_upstream)
        for start in range(0, half, tile):
            rows = slice(start, start + tile)
            turned[:, rows] = own_rows[rows, :].T
            turned[:, half + start : half + start + tile] = other_rows[rows, :].T

    for base, source in ((0, own_rows), (half, other_rows)):
        for start in range(0, half, tile):
            rows = slice(base + start, base + start + tile)
            hidden = dot(source[start : start + tile, :], up[...])
            active_grads = dot(out_grads[rows, :], down[...], ((1,), (1,)))
            low_active, slope = gelu_parts(hidden)
            active[rows, :] = low_active
            hidden_grads[rows, :] = (active_grads * slope).astype(BF16)
    up_grad[0] = dot(turned[...], hidden_grads[...]).astype(BF16)
    down_grad[0] = dot(active[...], out_grads[...], ((0,), (0,))).astype(BF16)


def params():
    return pltpu.CompilerParams(
        dimension_semantics=("arbitrary",), vmem_limit_bytes=VMEM_LIMIT
    )


def cost(flops, size):
    return pl.CostEstimate(flops=flops, bytes_accessed=size, transcendentals=0)


def attend(tokens, gain, weight, bias, count):
    length, width = tokens.shape
    group = bias.shape[0]
    size = weight.shape[1] // group
    tile = length // count
    return pl.pallas_call(
        attend_kernel,
        grid=(group,),
        in_specs=[
            pl.BlockSpec((length, width), lambda h: (0, 0)),
            pl.BlockSpec((1, width), lambda h: (0, 0)),
            pl.BlockSpec((3, size, width), lambda h: (0, h, 0)),
            pl.BlockSpec((1, 1, length + tile), lambda h: (h, 0, 0)),
        ],
        out_specs=[
            pl.BlockSpec((length, width), lambda h: (0, 0)),
            pl.BlockSpec((3, size, length), lambda h: (0, h, 0)),
            pl.BlockSpec((count, size, tile), lambda h: (0, h, 0)),
            pl.BlockSpec((1, size, length), lambda h: (h, 0, 0)),
            pl.BlockSpec((1, 1, length), lambda h: (h, 0, 0)),
        ],
        out_shape=[
            jax.ShapeDtypeStruct((length, width), BF16),
            jax.ShapeDtypeStruct((3, group * size, length), BF16),
            jax.ShapeDtypeStruct((count, group * size, tile), BF16),
            jax.ShapeDtypeStruct((group, size, length), F32),
            jax.ShapeDtypeStruct((group, 1, length), F32),
        ],
        scratch_shapes=[pltpu.VMEM((length, tile), F32)],
        compiler_params=params(),
        cost_estimate=cost(14 * length * width * size * group, 8 * length * width),
        name="attend",
    )(tokens, gain, weight, bias)


def attend_back(qkv, normed, bias, log_total, exact, grads_in):
    length, width = normed.shape
    count, _, tile = grads_in.shape
    group, size, _ = exact.shape
    return pl.pallas_call(
        attend_back_kernel,
        grid=(group,),
        in_specs=[
            pl.BlockSpec((3, size, length), lambda h: (0, h, 0)),
            pl.BlockSpec((length, width), lambda h: (0, 0)),
            pl.BlockSpec((1, 1, length + tile), lambda h: (h, 0, 0)),
            pl.BlockSpec((1, 1, length), lambda h: (h, 0, 0)),
            pl.BlockSpec((1, size, length), lambda h: (h, 0, 0)),
            pl.BlockSpec((count, size, tile), lambda h: (0, h, 0)),
        ],
        out_specs=[
            pl.BlockSpec((count, 3, size, tile), lambda h: (0, 0, h, 0)),
            pl.BlockSpec((3, size, width), lambda h: (0, h, 0)),
            pl.BlockSpec((1, 1, length + tile), lambda h: (h, 0, 0)),
        ],
        out_shape=[
            jax.ShapeDtypeStruct((count, 3, group * size, tile), BF16),
            jax.ShapeDtypeStruct((3, group * size, width), BF16),
            jax.ShapeDtypeStruct((group, 1, length + tile), F32),
        ],
        scratch_shapes=[
            pltpu.VMEM((count, tile, tile), F32),
            pltpu.VMEM((tile, tile), F32),
            pltpu.VMEM((count, tile, size), F32),
            pltpu.VMEM((count, tile, size), F32),
            pltpu.VMEM((count, size, tile), F32),
        ],
        compiler_params=params(),
        cost_estimate=cost(18 * length * width * size * group, 8 * length * width),
        name="attend_back",
    )(qkv, normed, bias, log_total, exact, grads_in)


def expert(rows_in, upstream, gate, up, down):
    rows, width = rows_in.shape
    hidden = up.shape[1]
    lanes, _, capacity = gate.shape
    return pl.pallas_call(
        expert_kernel,
        grid=(hidden // FF_TILE,),
        in_specs=[
            pl.BlockSpec((rows, width), lambda f: (0, 0)),
            pl.BlockSpec(upstream.shape, lambda f: (0, 0, 0)),
            pl.BlockSpec(gate.shape, lambda f: (0, 0, 0)),
            pl.BlockSpec((width, FF_TILE), lambda f: (0, f)),
            pl.BlockSpec((FF_TILE, width), lambda f: (f, 0)),
        ],
        out_specs=[
            pl.BlockSpec((rows, width), lambda f: (0, 0)),
            pl.BlockSpec((lanes, capacity + SPARE, width), lambda f: (0, 0, 0)),
        ],
        out_shape=[
            jax.ShapeDtypeStruct((rows, width), BF16),
            jax.ShapeDtypeStruct((lanes, capacity + SPARE, width), BF16),
        ],
        scratch_shapes=[
            pltpu.VMEM((rows, width), BF16),
            pltpu.VMEM((rows, width), F32),
            pltpu.VMEM((rows, 128), F32),
            pltpu.VMEM((rows, width), F32),
        ],
        compiler_params=params(),
        cost_estimate=cost(10 * rows * width * hidden, 4 * width * hidden),
        name="expert",
    )(rows_in, upstream, gate, up, down)


def expert_grads(index, own_rows, other_rows, own_upstream, other_upstream, own_gate, other_gate, up, down, count, steps):
    half, width = own_rows.shape
    hidden = up.shape[1]
    share = hidden // count
    whole = pl.BlockSpec((half, width), lambda s, i: (0, 0))
    slots = pl.BlockSpec(own_upstream.shape, lambda s, i: (0, 0, 0))
    gates = pl.BlockSpec(own_gate.shape, lambda s, i: (0, 0, 0))
    return pl.pallas_call(
        expert_grads_kernel,
        grid_spec=pltpu.PrefetchScalarGridSpec(
            num_scalar_prefetch=1,
            grid=(steps,),
            in_specs=[
                whole,
                whole,
                slots,
                slots,
                gates,
                gates,
                pl.BlockSpec((width, share), lambda s, i: (0, i[0] + s)),
                pl.BlockSpec((share, width), lambda s, i: (i[0] + s, 0)),
            ],
            out_specs=[
                pl.BlockSpec((1, width, share), lambda s, i: (s, 0, 0)),
                pl.BlockSpec((1, share, width), lambda s, i: (s, 0, 0)),
            ],
            scratch_shapes=[
                pltpu.VMEM((width, 2 * half), BF16),
                pltpu.VMEM((2 * half, width), BF16),
                pltpu.VMEM((2 * half, share), BF16),
                pltpu.VMEM((2 * half, share), BF16),
            ],
        ),
        out_shape=[
            jax.ShapeDtypeStruct((steps, width, share), BF16),
            jax.ShapeDtypeStruct((steps, share, width), BF16),
        ],
        compiler_params=params(),
        cost_estimate=cost(16 * half * width * share * steps, 8 * half * width),
        name="expert_grads",
    )(index, own_rows, other_rows, own_upstream, other_upstream, own_gate, other_gate, up, down)


def assemble_kernel(
    bits, chunk, index, near, far, query, key, value,
    query_grad, key_grad, value_grad, proj_grad, small_sum, gain_sum,
):
    outer = bits[1:]
    lanes = 1 << len(bits)
    count, depth, half = near.shape[-3:]
    own = index[0]
    first = pl.program_id(0) == 0

    def block(lane, z):
        turn = own ^ lane
        steps = [lax.rem(turn // bit, 2) for bit in outer]
        places = [jnp.where(first, a, b) for a, b in zip(steps, steps[::-1])]
        side = lax.rem(turn // bits[0], 2) == 0
        at = (0, *places, z)
        return jnp.where(side, near[at], far[at]).astype(F32)

    order = []
    for i in range(lanes):
        lane = 0
        for j, bit in enumerate(bits):
            lane += bit * ((i >> (len(bits) - 1 - j)) & 1)
        order.append(lane)
    blocks = [[block(lane, z) for z in range(count)] for lane in order]
    part = chunk // 3
    share = depth - chunk - SPARE
    for i in range(lanes):
        total = blocks[i][0][chunk : chunk + SPARE]
        for z in range(1, count):
            total = total + blocks[i][z][chunk : chunk + SPARE]
        small_sum[i * SPARE : (i + 1) * SPARE, :] = total
    proj_grad[...] = jnp.concatenate(
        [blocks[i][z][chunk + SPARE :] for i in range(lanes) for z in range(count)], axis=0
    )
    total = None
    for j, (weight, grad) in enumerate(
        ((query, query_grad), (key, key_grad), (value, value_grad))
    ):
        rows = [
            blocks[i][z][j * part : (j + 1) * part] for z in range(count) for i in range(lanes)
        ]
        whole = jnp.concatenate(rows, axis=0)[: grad.shape[1]].T
        grad[...] = whole
        sums = jnp.sum(whole * weight[...].astype(F32), axis=1, keepdims=True)
        total = sums if total is None else total + sums
    gain_sum[...] = total


def assemble(index, near, far, query, key, value, bits, chunk):
    shape = near.shape
    half = shape[-1]
    width = query.shape[0]
    lanes = 1 << len(bits)
    rows = pl.BlockSpec((half, width), lambda s, i: (s, 0))
    cols = pl.BlockSpec((width, half), lambda s, i: (0, s))
    pack = pl.BlockSpec((1,) + shape[1:], lambda s, i: (s,) + (0,) * (len(shape) - 1))
    return pl.pallas_call(
        partial(assemble_kernel, bits, chunk),
        grid_spec=pltpu.PrefetchScalarGridSpec(
            num_scalar_prefetch=1,
            grid=(shape[0],),
            in_specs=[pack, pack, rows, rows, rows],
            out_specs=[
                rows,
                rows,
                rows,
                cols,
                pl.BlockSpec((lanes * SPARE, half), lambda s, i: (0, s)),
                pl.BlockSpec((half, 1), lambda s, i: (s, 0)),
            ],
        ),
        out_shape=[jax.ShapeDtypeStruct((width, width), F32)] * 4
        + [
            jax.ShapeDtypeStruct((lanes * SPARE, width), F32),
            jax.ShapeDtypeStruct((width, 1), F32),
        ],
        compiler_params=params(),
        name="assemble",
    )(index, near, far, query, key, value)


def token_back_kernel(
    returns, dispatch, gates, chosen, middle, cotangent, gain, routed, router, proj,
    middle_grads, branch_grads, mixed_grads, gain_grad, router_grad,
):
    experts, depth, width = returns.shape
    capacity = depth - SPARE
    grads = None
    columns = []
    for i in range(experts):
        select = dispatch[:, i * capacity : (i + 1) * capacity]
        part = dot(select, returns[i, :capacity, :])
        grads = part if grads is None else grads + part
        lines = returns[i, capacity:, :].astype(F32)
        line = (lines[0:1] + lines[1:2])[:, :capacity]
        columns.append(jnp.sum(select.astype(F32) * line, axis=1, keepdims=True))
    total = columns[0]
    for column in columns[1:]:
        total = total + column
    logit_grads = []
    for i in range(experts):
        grad = (columns[i] - gates[:, i : i + 1] * total) * chosen[:, i : i + 1]
        logit_grads.append(grad)
        grads = grads + grad * router[i : i + 1, :]
        router_grad[i : i + 1, :] = jnp.sum(grad * routed[...].astype(F32), axis=0, keepdims=True)
    value = middle[...]
    scale = lax.rsqrt(jnp.mean(value * value, axis=1, keepdims=True) + EPSILON)
    normal = value * scale
    gain_grad[...] = jnp.sum(grads * normal, axis=0, keepdims=True)
    inner = grads * gain[...]
    back = scale * (inner - normal * jnp.mean(inner * normal, axis=1, keepdims=True))
    result = cotangent[...].astype(F32) + back
    middle_grads[...] = result
    low = result.astype(BF16)
    branch_grads[...] = low
    mixed_grads[...] = dot(proj[...], low, ((1,), (1,))).astype(BF16)


def token_back(returns, dispatch, gates, chosen, middle, cotangent, gain, routed, router, proj):
    rows, width = middle.shape
    return pl.pallas_call(
        token_back_kernel,
        out_shape=[
            jax.ShapeDtypeStruct((rows, width), F32),
            jax.ShapeDtypeStruct((rows, width), BF16),
            jax.ShapeDtypeStruct((width, rows), BF16),
            jax.ShapeDtypeStruct((1, width), F32),
            jax.ShapeDtypeStruct(router.shape, F32),
        ],
        compiler_params=pltpu.CompilerParams(vmem_limit_bytes=VMEM_LIMIT),
        name="token_back",
    )(returns, dispatch, gates, chosen, middle, cotangent, gain, routed, router, proj)


def chosen_softmax(logits, chosen, axis):
    peak = jnp.max(jnp.where(chosen, logits, -jnp.inf), axis=axis, keepdims=True)
    peak = jnp.where(peak > -jnp.inf, peak, 0.0)
    parts = jnp.where(chosen, jnp.exp(jnp.where(chosen, logits, peak) - peak), 0.0)
    total = jnp.sum(parts, axis=axis, keepdims=True)
    return parts / jnp.where(total > 0.0, total, 1.0)


def to_experts(value):
    return exchange(value, "expert")


def to_context(value):
    return exchange(value, "context")


def exchange(value, axis):
    return lax.all_to_all(value, axis, split_axis=0, concat_axis=0)


def exchange_steps(value, axis, send):
    count = lax.axis_size(axis)
    here = lax.axis_index(axis)
    whole = jnp.zeros_like(value)
    for step in sorted(range(count), key=lambda k: (k != 0, -min(k, count - k))):
        target, source, part = send(here, step)
        piece = lax.dynamic_slice_in_dim(value, target, 1, 0)
        whole = lax.dynamic_update_slice_in_dim(whole, part(piece) if step else piece, source, 0)
    return whole


def expert_steps(value):
    def send(here, step):
        return here ^ step, here ^ step, lambda piece: swap(piece, "expert", step)

    return exchange_steps(value, "expert", send)


def context_steps(value, arrivals=None):
    count = lax.axis_size("context")

    def send(here, step):
        target, source = lax.rem(here + step, count), lax.rem(here - step + count, count)

        def part(piece):
            piece = shift(piece, "context", step)
            if arrivals is not None:
                arrivals.append(piece)
            return piece

        return target, source, part

    return exchange_steps(value, "context", send)


def shards(
    tokens,
    gain_attn,
    w_query,
    w_key,
    w_value,
    w_proj,
    bias_table,
    gain_moe,
    w_router,
    w_up,
    w_down,
    routes,
    bucket_ids,
    cotangent,
):
    rows, width = tokens.shape
    size = width // HEADS
    experts = w_router.shape[1]
    buckets = bias_table.shape[0]
    picks = routes.shape[1]
    capacity = 2 * rows * picks // experts
    slots = experts * capacity
    count = lax.axis_size("context")
    lanes = lax.axis_size("expert")
    here = lax.axis_index("context")
    own = lax.axis_index("expert")
    length = rows * count
    group = -(-HEADS // count)
    held = group * size
    extra = count * group - HEADS

    token_parts = ring_parts(tokens, "context")

    expert_ids = jnp.arange(experts, dtype=jnp.int32)
    order = jnp.arange(rows, dtype=jnp.int32)
    earlier = (order[:, None] > order[None, :]).astype(BF16)

    def routing(block):
        chosen = jnp.any(block[:, :, None] == expert_ids[None, None, :], axis=1)
        member = chosen.astype(BF16)
        place = dot(earlier, member).astype(jnp.int32)
        dispatch = (
            (place[:, :, None] == jnp.arange(capacity, dtype=jnp.int32)[None, None, :])
            & chosen[:, :, None]
        ).astype(BF16)
        return chosen, member, dispatch.reshape(rows, slots)

    chosen, member, dispatch = routing(routes)

    def slots_of(dispatch, block):
        sent = dot(dispatch, block, ((0,), (0,))).astype(BF16)
        return sent.reshape(experts, capacity, width)

    def upstream_sent(member, dispatch, block):
        choices = dot(member, dispatch, ((0,), (0,))).astype(BF16)
        choices = jnp.transpose(choices.reshape(experts, experts, capacity), (1, 0, 2))
        choices = jnp.pad(choices, ((0, 0), (0, 0), (0, width - capacity)))
        return jnp.concatenate([slots_of(dispatch, block), choices], axis=1)

    partner = count // 2

    def head_rows(weight):
        whole = jnp.pad(weight, ((0, 0), (0, extra * size)))
        return lax.dynamic_slice_in_dim(whole, here * held, held, 1).T

    head_weights = jnp.stack([head_rows(w) for w in (w_query, w_key, w_value)])

    own_sent, head_weights = after(
        (upstream_sent(member, dispatch, cotangent), head_weights), token_parts[-1][1]
    )
    upstream_slots = to_experts(own_sent)
    sequence = in_order(token_parts, "context")
    cotangent_other, routes_other = after((cotangent, routes.T), sequence)
    cotangent_other = swap(cotangent_other, "context", partner)
    routes_other = swap(routes_other, "context", partner)

    bucket_match = (
        bucket_ids[:, None] == jnp.arange(buckets, dtype=jnp.int32)[None, :]
    ).astype(F32)
    per_distance = lax.dot_general(
        jnp.pad(bias_table, ((0, 0), (0, extra))), bucket_match, (((0,), (1,)), ((), ())),
        precision=HIGHEST,
    )
    bias = jnp.pad(
        lax.dynamic_slice_in_dim(per_distance, here * group, group, 0),
        ((0, 0), (rows, 0)),
        constant_values=MASKED,
    )[:, None, :]
    normed, qkv, mixed_parts, exact, log_total = attend(
        sequence, gain_attn[None, :], head_weights, bias, count
    )
    mixed_parts, upstream_slots, cotangent_other, routes_other = lax.optimization_barrier(
        (mixed_parts, upstream_slots, cotangent_other, routes_other)
    )
    unused, member_other, dispatch_other = routing(routes_other.T)
    upstream_other = to_experts(upstream_sent(member_other, dispatch_other, cotangent_other))
    mixed = context_steps(mixed_parts).reshape(count * held, rows)[:width]
    source = tokens.astype(F32)
    middle = source + dot(mixed, w_proj, ((0,), (0,)))
    moe_normal, moe_scale = normalize(middle, gain_moe)
    routed = moe_normal.astype(BF16)

    logits = dot(routed, w_router)
    gates = chosen_softmax(logits, chosen, 1)

    def gates_of(received, upstream):
        choices = jnp.moveaxis(upstream[:, capacity:, :capacity], 1, 0) > 0.5
        slot_logits = dot(w_router, received, ((0,), (1,))).reshape(experts, lanes, capacity)
        slot_gates = chosen_softmax(slot_logits, choices, 0)
        return lax.dynamic_index_in_dim(slot_gates, own, 0, keepdims=False)[:, None, :]

    sent, upstream_other = lax.optimization_barrier((slots_of(dispatch, routed), upstream_other))
    received = to_experts(sent).reshape(slots, width)
    routed_other = swap(routed, "context", partner)
    received, routed_other = lax.optimization_barrier((received, routed_other))
    received_other = to_experts(slots_of(dispatch_other, routed_other)).reshape(slots, width)
    slot_gate = gates_of(received, upstream_slots)
    expert_out, row_grads = expert(received, upstream_slots, slot_gate, w_up[0], w_down[0])
    row_grads, received_other = lax.optimization_barrier((row_grads, received_other))
    row_returns = to_experts(row_grads)

    quarter = partner // 2
    mine = lax.rem(here // quarter, 2)
    first = (here // partner) * partner
    other_gate = gates_of(received_other, upstream_other)

    def gradients(start, hold):
        return expert_grads(
            after(start, hold)[None],
            received,
            received_other,
            upstream_slots,
            upstream_other,
            slot_gate,
            other_gate,
            w_up[0],
            w_down[0],
            count,
            quarter,
        )

    up_sent, down_sent = gradients(first + (1 - mine) * quarter, row_grads)
    up_kept, down_kept = gradients(first + mine * quarter, down_sent)
    row_returns, down_sent, up_kept, down_kept = lax.optimization_barrier(
        (row_returns, down_sent, up_kept, down_kept)
    )
    up_arrived = swap(up_sent, "context", quarter)
    low_bits = [1 << i for i in range(quarter.bit_length() - 1)][::-1]
    spread = dispatch.reshape(rows, experts, capacity).astype(F32)
    middle_grads, branch_grads, mixed_grads, gain_moe_grad, router_grad = token_back(
        row_returns,
        dispatch,
        gates,
        chosen.astype(F32),
        middle,
        cotangent,
        gain_moe[None, :],
        routed,
        w_router.astype(F32).T,
        w_proj,
    )
    arrivals = []
    grads_in = context_steps(
        jnp.pad(mixed_grads, ((0, extra * size), (0, 0))).reshape(count, held, rows),
        arrivals,
    )
    bits = bit_orders(lanes)
    out_returns = to_experts(after(expert_out, arrivals[0]).reshape(experts, capacity, width))
    grads_in, up_arrived = lax.optimization_barrier((grads_in, up_arrived))
    proj_part = dot(mixed, branch_grads).astype(BF16).reshape(lanes, width // lanes, width)
    proj_part = halve_sum(proj_part, "expert", bits).astype(BF16)
    proj_part = context_steps(proj_part.reshape(count, width // (lanes * count), width))
    proj_rows = jnp.sum(proj_part.astype(F32), axis=0).astype(BF16)

    grads_out, weight_grads, diagonals = attend_back(
        qkv, normed, bias, log_total, exact, grads_in
    )
    weight_grads, out_returns = lax.optimization_barrier((weight_grads, out_returns))
    table_part = jnp.dot(diagonals[:, 0, rows:], bucket_match, precision=HIGHEST)
    table_line = lax.dynamic_update_slice(
        jnp.zeros((count * group, buckets), F32), table_part, (here * group, 0)
    )[:HEADS].reshape(1, HEADS * buckets)
    table_line = jnp.pad(table_line, ((0, 0), (0, width - HEADS * buckets)))
    small = jnp.concatenate([router_grad, gain_moe_grad, table_line], axis=0)
    small = jnp.pad(small, ((0, lanes * SPARE - small.shape[0]), (0, 0))).astype(BF16)
    chunk = 3 * held // lanes
    pack = jnp.concatenate(
        [
            jnp.moveaxis(weight_grads.reshape(3, lanes, held // lanes, width), 1, 0).reshape(
                lanes, chunk, width
            ),
            small.reshape(lanes, SPARE, width),
        ],
        axis=1,
    )
    pack = halve_sum(pack, "expert", bits).astype(BF16)
    arrived = context_steps(grads_out)
    pack = jnp.concatenate([pack, proj_rows], axis=0)
    pack = in_order(ring_parts(pack[None], "context"), "context")
    pack, arrived = lax.optimization_barrier((pack, arrived))
    down_arrived = swap(after(down_sent, pack), "context", quarter)
    normed_grads = 0.0
    for j, weight in enumerate((w_query, w_key, w_value)):
        part = arrived[:, j].reshape(count * held, rows)[:width]
        normed_grads = normed_grads + dot(part, weight, ((0,), (1,)))
    attention_scale = lax.rsqrt(jnp.mean(source * source, axis=1, keepdims=True) + EPSILON)
    token_norm_grads, unused = normalize_back(normed_grads, source, attention_scale, gain_attn)
    token_grads = (middle_grads + token_norm_grads).astype(BF16)
    up_grad = up_kept.astype(F32) + up_arrived.astype(F32)
    up_grad = halve_sum(up_grad, "context", low_bits, BF16)
    gated = (spread * gates[:, :, None]).reshape(rows, slots)
    output = middle + jnp.dot(
        gated, out_returns.reshape(slots, width).astype(F32), precision=HIGHEST
    )
    half = width // 2
    sides = (bits[:0:-1], bits[1:])
    parts = [
        double_gather(part, "expert", order[:1])
        for part, order in zip((pack[:, :, :half], pack[:, :, half:]), sides)
    ]
    parts, token_grads, up_grad, output = lax.optimization_barrier(
        (parts, token_grads, up_grad, output)
    )
    near = jnp.stack(
        [double_gather(part, "expert", order[1:]) for part, order in zip(parts, sides)]
    )
    near, down_arrived = lax.optimization_barrier((near, down_arrived))
    far = swap(near, "expert", bits[0])
    down_grad = down_kept.astype(F32) + down_arrived.astype(F32)
    down_grad = halve_sum(down_grad, "context", low_bits, BF16)
    grad_query, grad_key, grad_value, grad_proj, small, gain_attn_total = assemble(
        own[None], near, far, w_query, w_key, w_value, bits, chunk
    )
    gain_attn_total = gain_attn_total[:, 0] / gain_attn
    router_total = small[:experts].T
    gain_moe_total = small[experts]
    table_total = small[experts + 1, : HEADS * buckets].reshape(HEADS, buckets).T
    return (
        output.astype(BF16),
        token_grads,
        gain_attn_total,
        grad_query,
        grad_key,
        grad_value,
        grad_proj,
        table_total,
        gain_moe_total,
        router_total,
        up_grad[None],
        down_grad[None],
    )


def solution(mesh):
    return jax.shard_map(
        shards,
        mesh=mesh,
        in_specs=(
            P(("expert", "context"), None),
            P(),
            P(),
            P(),
            P(),
            P(),
            P(),
            P(),
            P(),
            P("expert", None, None),
            P("expert", None, None),
            P(("expert", "context"), None),
            P(),
            P(("expert", "context"), None),
        ),
        out_specs=(
            P(("expert", "context"), None),
            P(("expert", "context"), None),
            P(),
            P(),
            P(),
            P(),
            P(),
            P(),
            P(),
            P(),
            P("expert", None, "context"),
            P("expert", "context", None),
        ),
        check_vma=False,
    )
```

```python
from functools import partial

import jax
import jax.numpy as jnp
from jax import lax
from jax.experimental import pallas as pl
from jax.experimental.pallas import tpu as pltpu
from jax.sharding import PartitionSpec as P

HEADS = 12
EPSILON = 1e-06
HIGHEST = lax.Precision.HIGHEST
MASKED = -1000000000.0
F32 = jnp.float32
BF16 = jnp.bfloat16
VMEM_LIMIT = 56 * 1024 * 1024
FF_TILE = 512
SPARE = 8
ROW_TILE = 512


def dot(left, right, dims=((1,), (0,))):
    return lax.dot_general(left, right, (dims, ((), ())), preferred_element_type=F32)


def normalize(value, gain):
    scale = lax.rsqrt(jnp.mean(value * value, axis=1, keepdims=True) + EPSILON)
    return (value * scale * gain, scale)


def normalize_back(grad, value, scale, gain):
    normal = value * scale
    inner = grad * gain
    gain_grad = jnp.sum(grad * normal, axis=0)
    value_grad = scale * (inner - normal * jnp.mean(inner * normal, axis=1, keepdims=True))
    return (value_grad, gain_grad)


def shift(value, axis, step):
    count = lax.axis_size(axis)
    return lax.ppermute(value, axis, [(i, (i + step) % count) for i in range(count)])


def swap(value, axis, bit):
    count = lax.axis_size(axis)
    return lax.ppermute(value, axis, [(i, i ^ bit) for i in range(count)])


def after(value, *others):
    return lax.optimization_barrier((value, others))[0]


def ring_parts(value, axis, hold=None):
    count = lax.axis_size(axis)
    parts = [(0, value)]
    right = left = value
    for step in range(1, count // 2 + 1):
        if step == 2 and hold is not None:
            right, left = after((right, left), hold)
        right = shift(right, axis, 1)
        parts.append((step, right))
        if step <= (count - 1) // 2:
            left = shift(left, axis, -1)
            parts.append((count - step, left))
    return parts


def in_order(parts, axis):
    count = lax.axis_size(axis)
    here = lax.axis_index(axis)
    value = parts[0][1]
    size = value.shape[0]
    whole = jnp.zeros((count * size,) + value.shape[1:], value.dtype)
    for step, part in parts:
        whole = lax.dynamic_update_slice_in_dim(
            whole, part, lax.rem(here - step + count, count) * size, 0
        )
    return whole


def bit_orders(count):
    bits = [1 << i for i in range(count.bit_length() - 1)]
    return bits[:1] + bits[:0:-1]


def halve_sum(value, axis, bits, low=BF16):
    here = lax.axis_index(axis)
    for bit in bits:
        pair = value.reshape((2, value.shape[0] // 2) + value.shape[1:])
        mine = lax.rem(here // bit, 2)
        kept = lax.dynamic_index_in_dim(pair, mine, 0, keepdims=False)
        sent = lax.dynamic_index_in_dim(pair, 1 - mine, 0, keepdims=False).astype(low)
        value = kept.astype(F32) + swap(sent, axis, bit).astype(F32)
    return value[0]


def double_gather(value, axis, order):
    for bit in order:
        value = jnp.stack([value, swap(value, axis, bit)])
    return value


def attend_kernel(tokens, gain, weight, bias, normed, qkv, mixed, exact, log_total, tiles):
    length = tokens.shape[0]
    count, size, tile = mixed.shape

    @pl.when(pl.program_id(0) == 0)
    def _():
        def body(i, carry):
            part = pl.ds(i * tile, tile)
            normal, unused = normalize(tokens[part, :].astype(F32), gain[...])
            normed[part, :] = normal.astype(BF16)
            return carry

        lax.fori_loop(0, count, body, 0)

    weight_all = weight[...].reshape(3 * size, weight.shape[2])
    key_parts = []
    for i in range(count):
        part = dot(weight_all, normed[i * tile : (i + 1) * tile, :], ((1,), (1,)))
        low = part.astype(BF16)
        for j in range(3):
            qkv[j, :, i * tile : (i + 1) * tile] = low[j * size : (j + 1) * size, :]
        key_parts.append(part[size : 2 * size, :].T.astype(BF16))
        wide = jnp.broadcast_to(bias[0, :, i * tile : (i + 2) * tile], (tile, 2 * tile))
        turned = pltpu.roll(wide, tile, 1, stride=1, stride_axis=0)
        tiles[(count - 1 - i) * tile : (count - i) * tile, :] = turned[:, :tile]
    keys = jnp.concatenate(key_parts, axis=0)
    factor = size ** (-0.5)
    for i in range(count):
        cols = slice(i * tile, (i + 1) * tile)
        many = (i + 1) * tile
        scores = dot(keys[:many], qkv[0, :, cols]) * factor + tiles[length - many :, :]
        peak = jnp.max(scores, axis=0, keepdims=True)
        weights = jnp.exp(scores - peak)
        total = jnp.sum(weights, axis=0, keepdims=True)
        result = dot(qkv[2, :, :many], weights.astype(BF16)) * (1.0 / total)
        exact[0, :, cols] = result
        mixed[i, :, :] = result.astype(BF16)
        log_total[0, :, cols] = peak + jnp.log(total)


def fold(grid):
    tile = grid.shape[0]
    value = jnp.concatenate([jnp.zeros_like(grid), grid], axis=1)
    half = tile // 2
    while half >= 8:
        value = value[:half] + pltpu.roll(value[half:], 2 * tile - half, 1)
        half //= 2
    return value


def attend_back_kernel(
    qkv, normed, bias, log_total, exact, grads_in, grads, weight_grads, diagonals,
    tiles, sums, keys_acc, values_acc, query_acc,
):
    count, size, tile = grads_in.shape
    factor = size ** (-0.5)
    queries, values, outs, deltas = [], [], [], []
    keys = []
    for i in range(count):
        cols = slice(i * tile, (i + 1) * tile)
        queries.append(qkv[0, :, cols].astype(F32).T.astype(BF16))
        keys.append(qkv[1, :, cols].astype(F32).T.astype(BF16))
        values.append(qkv[2, :, cols].astype(F32).T.astype(BF16))
        out = grads_in[i].astype(F32)
        outs.append(out.T.astype(BF16))
        deltas.append(jnp.sum(out * exact[0, :, cols], axis=0, keepdims=True))
        wide = jnp.broadcast_to(bias[0, :, i * tile : (i + 2) * tile], (tile, 2 * tile))
        turned = pltpu.roll(wide, tile, 1, stride=1, stride_axis=0)
        tiles[i] = turned[:, :tile]
    for d in range(count):
        for j in range(count - d):
            i = j + d
            cols = slice(i * tile, (i + 1) * tile)
            scores = dot(keys[j], qkv[0, :, cols]) * factor + tiles[d]
            probs = jnp.exp(scores - log_total[0, :, cols])
            prob_grads = dot(values[j], grads_in[i])
            score_grads = probs * (prob_grads - deltas[i])
            low = score_grads.astype(BF16)
            value_part = dot(probs.astype(BF16), outs[i])
            key_part = dot(low, queries[i])
            query_part = dot(qkv[1, :, j * tile : (j + 1) * tile], low)
            if j == 0:
                sums[...] = score_grads
            else:
                sums[...] += score_grads
            if d == 0:
                values_acc[j] = value_part
                keys_acc[j] = key_part
                query_acc[i] = query_part
            else:
                values_acc[j] += value_part
                keys_acc[j] += key_part
                query_acc[i] += query_part
        rows = fold(sums[...])
        line = rows[0:1]
        for r in range(1, 8):
            line = line + pltpu.roll(rows[r : r + 1], 2 * tile - r, 1)
        if d == 0:
            diagonals[0, :, : 2 * tile] = line
        else:
            diagonals[0, :, d * tile : (d + 1) * tile] += line[:, :tile]
            diagonals[0, :, (d + 1) * tile : (d + 2) * tile] = line[:, tile:]
    total = None
    for i in range(count):
        query_part = (query_acc[i] * factor).astype(BF16)
        key_part = (keys_acc[i] * factor).T.astype(BF16)
        value_part = values_acc[i].T.astype(BF16)
        grads[i, 0] = query_part
        grads[i, 1] = key_part
        grads[i, 2] = value_part
        stacked = jnp.concatenate([query_part, key_part, value_part], axis=0)
        part = dot(stacked, normed[i * tile : (i + 1) * tile, :])
        total = part if total is None else total + part
    for j in range(3):
        weight_grads[j] = total[j * size : (j + 1) * size, :].astype(BF16)


def gelu_parts(hidden):
    below = 0.5 * (1.0 + lax.erf(hidden * (0.5**0.5)))
    density = jnp.exp(-0.5 * hidden * hidden) * 0.3989422804014327
    return (hidden * below).astype(BF16), below + hidden * density


def scaled_rows(target, start, gate, upstream):
    lanes, capacity = gate.shape[0], gate.shape[2]
    for i in range(lanes):
        column = jnp.broadcast_to(gate[i], (8, capacity)).T[:, :1]
        grads = column * upstream[i, :capacity, :].astype(F32)
        target[start + i * capacity : start + (i + 1) * capacity, :] = grads.astype(BF16)


def expert_kernel(rows_in, upstream, gate, up, down, outs, row_grads, out_grads, acc, sums, out_acc):
    step = pl.program_id(0)
    lanes, capacity = gate.shape[0], gate.shape[2]

    @pl.when(step == 0)
    def _():
        scaled_rows(out_grads, 0, gate, upstream)
        acc[...] = jnp.zeros_like(acc)
        out_acc[...] = jnp.zeros_like(out_acc)
        sums[...] = jnp.zeros_like(sums)

    hidden = dot(rows_in[...], up[...])
    active_grads = dot(out_grads[...], down[...], ((1,), (1,)))
    low_active, slope = gelu_parts(hidden)
    low_grads = (active_grads * slope).astype(BF16)
    out_acc[...] += dot(low_active, down[...])
    acc[...] += dot(low_grads, up[...], ((1,), (1,)))
    weighted = low_active.astype(F32) * active_grads
    part = weighted[:, :128]
    for i in range(1, weighted.shape[1] // 128):
        part = part + weighted[:, i * 128 : (i + 1) * 128]
    sums[...] += part

    @pl.when(step == pl.num_programs(0) - 1)
    def _():
        outs[...] = out_acc[...].astype(BF16)
        low = acc[...].astype(BF16)
        for i in range(lanes):
            rows = slice(i * capacity, (i + 1) * capacity)
            row_grads[i, :capacity, :] = low[rows, :]
            line = jnp.sum(sums[rows, :].T, axis=0, keepdims=True)
            high = line.astype(BF16).astype(F32)
            both = jnp.concatenate([high, line - high, jnp.zeros((SPARE - 2, capacity), F32)])
            row_grads[i, capacity:, :] = jnp.zeros((SPARE, row_grads.shape[2]), BF16)
            row_grads[i, capacity:, :capacity] = both.astype(BF16)


def expert_grads_kernel(
    index, own_rows, other_rows, own_upstream, other_upstream, own_gate, other_gate, up, down,
    up_grad, down_grad, turned, out_grads, active, hidden_grads,
):
    half = own_rows.shape[0]
    tile = min(ROW_TILE, half)

    @pl.when(pl.program_id(0) == 0)
    def _():
        scaled_rows(out_grads, 0, own_gate, own_upstream)
        scaled_rows(out_grads, half, other_gate, other_upstream)
        for start in range(0, half, tile):
            rows = slice(start, start + tile)
            turned[:, rows] = own_rows[rows, :].T
            turned[:, half + start : half + start + tile] = other_rows[rows, :].T

    for base, source in ((0, own_rows), (half, other_rows)):
        for start in range(0, half, tile):
            rows = slice(base + start, base + start + tile)
            hidden = dot(source[start : start + tile, :], up[...])
            active_grads = dot(out_grads[rows, :], down[...], ((1,), (1,)))
            low_active, slope = gelu_parts(hidden)
            active[rows, :] = low_active
            hidden_grads[rows, :] = (active_grads * slope).astype(BF16)
    up_grad[0] = dot(turned[...], hidden_grads[...]).astype(BF16)
    down_grad[0] = dot(active[...], out_grads[...], ((0,), (0,))).astype(BF16)


def params():
    return pltpu.CompilerParams(
        dimension_semantics=("arbitrary",), vmem_limit_bytes=VMEM_LIMIT
    )


def cost(flops, size):
    return pl.CostEstimate(flops=flops, bytes_accessed=size, transcendentals=0)


def attend(tokens, gain, weight, bias, count):
    length, width = tokens.shape
    group = bias.shape[0]
    size = weight.shape[1] // group
    tile = length // count
    return pl.pallas_call(
        attend_kernel,
        grid=(group,),
        in_specs=[
            pl.BlockSpec((length, width), lambda h: (0, 0)),
            pl.BlockSpec((1, width), lambda h: (0, 0)),
            pl.BlockSpec((3, size, width), lambda h: (0, h, 0)),
            pl.BlockSpec((1, 1, length + tile), lambda h: (h, 0, 0)),
        ],
        out_specs=[
            pl.BlockSpec((length, width), lambda h: (0, 0)),
            pl.BlockSpec((3, size, length), lambda h: (0, h, 0)),
            pl.BlockSpec((count, size, tile), lambda h: (0, h, 0)),
            pl.BlockSpec((1, size, length), lambda h: (h, 0, 0)),
            pl.BlockSpec((1, 1, length), lambda h: (h, 0, 0)),
        ],
        out_shape=[
            jax.ShapeDtypeStruct((length, width), BF16),
            jax.ShapeDtypeStruct((3, group * size, length), BF16),
            jax.ShapeDtypeStruct((count, group * size, tile), BF16),
            jax.ShapeDtypeStruct((group, size, length), F32),
            jax.ShapeDtypeStruct((group, 1, length), F32),
        ],
        scratch_shapes=[pltpu.VMEM((length, tile), F32)],
        compiler_params=params(),
        cost_estimate=cost(14 * length * width * size * group, 8 * length * width),
        name="attend",
    )(tokens, gain, weight, bias)


def attend_back(qkv, normed, bias, log_total, exact, grads_in):
    length, width = normed.shape
    count, _, tile = grads_in.shape
    group, size, _ = exact.shape
    return pl.pallas_call(
        attend_back_kernel,
        grid=(group,),
        in_specs=[
            pl.BlockSpec((3, size, length), lambda h: (0, h, 0)),
            pl.BlockSpec((length, width), lambda h: (0, 0)),
            pl.BlockSpec((1, 1, length + tile), lambda h: (h, 0, 0)),
            pl.BlockSpec((1, 1, length), lambda h: (h, 0, 0)),
            pl.BlockSpec((1, size, length), lambda h: (h, 0, 0)),
            pl.BlockSpec((count, size, tile), lambda h: (0, h, 0)),
        ],
        out_specs=[
            pl.BlockSpec((count, 3, size, tile), lambda h: (0, 0, h, 0)),
            pl.BlockSpec((3, size, width), lambda h: (0, h, 0)),
            pl.BlockSpec((1, 1, length + tile), lambda h: (h, 0, 0)),
        ],
        out_shape=[
            jax.ShapeDtypeStruct((count, 3, group * size, tile), BF16),
            jax.ShapeDtypeStruct((3, group * size, width), BF16),
            jax.ShapeDtypeStruct((group, 1, length + tile), F32),
        ],
        scratch_shapes=[
            pltpu.VMEM((count, tile, tile), F32),
            pltpu.VMEM((tile, tile), F32),
            pltpu.VMEM((count, tile, size), F32),
            pltpu.VMEM((count, tile, size), F32),
            pltpu.VMEM((count, size, tile), F32),
        ],
        compiler_params=params(),
        cost_estimate=cost(18 * length * width * size * group, 8 * length * width),
        name="attend_back",
    )(qkv, normed, bias, log_total, exact, grads_in)


def expert(rows_in, upstream, gate, up, down):
    rows, width = rows_in.shape
    hidden = up.shape[1]
    lanes, _, capacity = gate.shape
    return pl.pallas_call(
        expert_kernel,
        grid=(hidden // FF_TILE,),
        in_specs=[
            pl.BlockSpec((rows, width), lambda f: (0, 0)),
            pl.BlockSpec(upstream.shape, lambda f: (0, 0, 0)),
            pl.BlockSpec(gate.shape, lambda f: (0, 0, 0)),
            pl.BlockSpec((width, FF_TILE), lambda f: (0, f)),
            pl.BlockSpec((FF_TILE, width), lambda f: (f, 0)),
        ],
        out_specs=[
            pl.BlockSpec((rows, width), lambda f: (0, 0)),
            pl.BlockSpec((lanes, capacity + SPARE, width), lambda f: (0, 0, 0)),
        ],
        out_shape=[
            jax.ShapeDtypeStruct((rows, width), BF16),
            jax.ShapeDtypeStruct((lanes, capacity + SPARE, width), BF16),
        ],
        scratch_shapes=[
            pltpu.VMEM((rows, width), BF16),
            pltpu.VMEM((rows, width), F32),
            pltpu.VMEM((rows, 128), F32),
            pltpu.VMEM((rows, width), F32),
        ],
        compiler_params=params(),
        cost_estimate=cost(10 * rows * width * hidden, 4 * width * hidden),
        name="expert",
    )(rows_in, upstream, gate, up, down)


def expert_grads(index, own_rows, other_rows, own_upstream, other_upstream, own_gate, other_gate, up, down, count, steps):
    half, width = own_rows.shape
    hidden = up.shape[1]
    share = hidden // count
    whole = pl.BlockSpec((half, width), lambda s, i: (0, 0))
    slots = pl.BlockSpec(own_upstream.shape, lambda s, i: (0, 0, 0))
    gates = pl.BlockSpec(own_gate.shape, lambda s, i: (0, 0, 0))
    return pl.pallas_call(
        expert_grads_kernel,
        grid_spec=pltpu.PrefetchScalarGridSpec(
            num_scalar_prefetch=1,
            grid=(steps,),
            in_specs=[
                whole,
                whole,
                slots,
                slots,
                gates,
                gates,
                pl.BlockSpec((width, share), lambda s, i: (0, i[0] + s)),
                pl.BlockSpec((share, width), lambda s, i: (i[0] + s, 0)),
            ],
            out_specs=[
                pl.BlockSpec((1, width, share), lambda s, i: (s, 0, 0)),
                pl.BlockSpec((1, share, width), lambda s, i: (s, 0, 0)),
            ],
            scratch_shapes=[
                pltpu.VMEM((width, 2 * half), BF16),
                pltpu.VMEM((2 * half, width), BF16),
                pltpu.VMEM((2 * half, share), BF16),
                pltpu.VMEM((2 * half, share), BF16),
            ],
        ),
        out_shape=[
            jax.ShapeDtypeStruct((steps, width, share), BF16),
            jax.ShapeDtypeStruct((steps, share, width), BF16),
        ],
        compiler_params=params(),
        cost_estimate=cost(16 * half * width * share * steps, 8 * half * width),
        name="expert_grads",
    )(index, own_rows, other_rows, own_upstream, other_upstream, own_gate, other_gate, up, down)


def assemble_kernel(
    bits, chunk, index, near, far, query, key, value,
    query_grad, key_grad, value_grad, proj_grad, small_sum, gain_sum,
):
    outer = bits[1:]
    lanes = 1 << len(bits)
    count, depth, half = near.shape[-3:]
    own = index[0]
    first = pl.program_id(0) == 0

    def block(lane, z):
        turn = own ^ lane
        steps = [lax.rem(turn // bit, 2) for bit in outer]
        places = [jnp.where(first, a, b) for a, b in zip(steps, steps[::-1])]
        side = lax.rem(turn // bits[0], 2) == 0
        at = (0, *places, z)
        return jnp.where(side, near[at], far[at]).astype(F32)

    order = []
    for i in range(lanes):
        lane = 0
        for j, bit in enumerate(bits):
            lane += bit * ((i >> (len(bits) - 1 - j)) & 1)
        order.append(lane)
    blocks = [[block(lane, z) for z in range(count)] for lane in order]
    part = chunk // 3
    share = depth - chunk - SPARE
    for i in range(lanes):
        total = blocks[i][0][chunk : chunk + SPARE]
        for z in range(1, count):
            total = total + blocks[i][z][chunk : chunk + SPARE]
        small_sum[i * SPARE : (i + 1) * SPARE, :] = total
    proj_grad[...] = jnp.concatenate(
        [blocks[i][z][chunk + SPARE :] for i in range(lanes) for z in range(count)], axis=0
    )
    total = None
    for j, (weight, grad) in enumerate(
        ((query, query_grad), (key, key_grad), (value, value_grad))
    ):
        rows = [
            blocks[i][z][j * part : (j + 1) * part] for z in range(count) for i in range(lanes)
        ]
        whole = jnp.concatenate(rows, axis=0)[: grad.shape[1]].T
        grad[...] = whole
        sums = jnp.sum(whole * weight[...].astype(F32), axis=1, keepdims=True)
        total = sums if total is None else total + sums
    gain_sum[...] = total


def assemble(index, near, far, query, key, value, bits, chunk):
    shape = near.shape
    half = shape[-1]
    width = query.shape[0]
    lanes = 1 << len(bits)
    rows = pl.BlockSpec((half, width), lambda s, i: (s, 0))
    cols = pl.BlockSpec((width, half), lambda s, i: (0, s))
    pack = pl.BlockSpec((1,) + shape[1:], lambda s, i: (s,) + (0,) * (len(shape) - 1))
    return pl.pallas_call(
        partial(assemble_kernel, bits, chunk),
        grid_spec=pltpu.PrefetchScalarGridSpec(
            num_scalar_prefetch=1,
            grid=(shape[0],),
            in_specs=[pack, pack, rows, rows, rows],
            out_specs=[
                rows,
                rows,
                rows,
                cols,
                pl.BlockSpec((lanes * SPARE, half), lambda s, i: (0, s)),
                pl.BlockSpec((half, 1), lambda s, i: (s, 0)),
            ],
        ),
        out_shape=[jax.ShapeDtypeStruct((width, width), F32)] * 4
        + [
            jax.ShapeDtypeStruct((lanes * SPARE, width), F32),
            jax.ShapeDtypeStruct((width, 1), F32),
        ],
        compiler_params=params(),
        name="assemble",
    )(index, near, far, query, key, value)


def token_back_kernel(
    returns, dispatch, gates, chosen, middle, cotangent, gain, routed, router, proj,
    middle_grads, branch_grads, mixed_grads, gain_grad, router_grad,
):
    experts, depth, width = returns.shape
    capacity = depth - SPARE
    grads = None
    columns = []
    for i in range(experts):
        select = dispatch[:, i * capacity : (i + 1) * capacity]
        part = dot(select, returns[i, :capacity, :])
        grads = part if grads is None else grads + part
        lines = returns[i, capacity:, :].astype(F32)
        line = (lines[0:1] + lines[1:2])[:, :capacity]
        columns.append(jnp.sum(select.astype(F32) * line, axis=1, keepdims=True))
    total = columns[0]
    for column in columns[1:]:
        total = total + column
    logit_grads = []
    for i in range(experts):
        grad = (columns[i] - gates[:, i : i + 1] * total) * chosen[:, i : i + 1]
        logit_grads.append(grad)
        grads = grads + grad * router[i : i + 1, :]
        router_grad[i : i + 1, :] = jnp.sum(grad * routed[...].astype(F32), axis=0, keepdims=True)
    value = middle[...]
    scale = lax.rsqrt(jnp.mean(value * value, axis=1, keepdims=True) + EPSILON)
    normal = value * scale
    gain_grad[...] = jnp.sum(grads * normal, axis=0, keepdims=True)
    inner = grads * gain[...]
    back = scale * (inner - normal * jnp.mean(inner * normal, axis=1, keepdims=True))
    result = cotangent[...].astype(F32) + back
    middle_grads[...] = result
    low = result.astype(BF16)
    branch_grads[...] = low
    mixed_grads[...] = dot(proj[...], low, ((1,), (1,))).astype(BF16)


def token_back(returns, dispatch, gates, chosen, middle, cotangent, gain, routed, router, proj):
    rows, width = middle.shape
    return pl.pallas_call(
        token_back_kernel,
        out_shape=[
            jax.ShapeDtypeStruct((rows, width), F32),
            jax.ShapeDtypeStruct((rows, width), BF16),
            jax.ShapeDtypeStruct((width, rows), BF16),
            jax.ShapeDtypeStruct((1, width), F32),
            jax.ShapeDtypeStruct(router.shape, F32),
        ],
        compiler_params=pltpu.CompilerParams(vmem_limit_bytes=VMEM_LIMIT),
        name="token_back",
    )(returns, dispatch, gates, chosen, middle, cotangent, gain, routed, router, proj)


def chosen_softmax(logits, chosen, axis):
    peak = jnp.max(jnp.where(chosen, logits, -jnp.inf), axis=axis, keepdims=True)
    peak = jnp.where(peak > -jnp.inf, peak, 0.0)
    parts = jnp.where(chosen, jnp.exp(jnp.where(chosen, logits, peak) - peak), 0.0)
    total = jnp.sum(parts, axis=axis, keepdims=True)
    return parts / jnp.where(total > 0.0, total, 1.0)


def to_experts(value):
    return exchange(value, "expert")


def to_context(value):
    return exchange(value, "context")


def exchange(value, axis):
    return lax.all_to_all(value, axis, split_axis=0, concat_axis=0)


def exchange_steps(value, axis, send):
    count = lax.axis_size(axis)
    here = lax.axis_index(axis)
    whole = jnp.zeros_like(value)
    for step in sorted(range(count), key=lambda k: (k != 0, -min(k, count - k))):
        target, source, part = send(here, step)
        piece = lax.dynamic_slice_in_dim(value, target, 1, 0)
        whole = lax.dynamic_update_slice_in_dim(whole, part(piece) if step else piece, source, 0)
    return whole


def expert_steps(value):
    def send(here, step):
        return here ^ step, here ^ step, lambda piece: swap(piece, "expert", step)

    return exchange_steps(value, "expert", send)


def context_steps(value, arrivals=None):
    count = lax.axis_size("context")

    def send(here, step):
        target, source = lax.rem(here + step, count), lax.rem(here - step + count, count)

        def part(piece):
            piece = shift(piece, "context", step)
            if arrivals is not None:
                arrivals.append(piece)
            return piece

        return target, source, part

    return exchange_steps(value, "context", send)


def shards(
    tokens,
    gain_attn,
    w_query,
    w_key,
    w_value,
    w_proj,
    bias_table,
    gain_moe,
    w_router,
    w_up,
    w_down,
    routes,
    bucket_ids,
    cotangent,
):
    rows, width = tokens.shape
    size = width // HEADS
    experts = w_router.shape[1]
    buckets = bias_table.shape[0]
    picks = routes.shape[1]
    capacity = 2 * rows * picks // experts
    slots = experts * capacity
    count = lax.axis_size("context")
    lanes = lax.axis_size("expert")
    here = lax.axis_index("context")
    own = lax.axis_index("expert")
    length = rows * count
    group = -(-HEADS // count)
    held = group * size
    extra = count * group - HEADS

    token_parts = ring_parts(tokens, "context")

    expert_ids = jnp.arange(experts, dtype=jnp.int32)
    order = jnp.arange(rows, dtype=jnp.int32)
    earlier = (order[:, None] > order[None, :]).astype(BF16)

    def routing(block):
        chosen = jnp.any(block[:, :, None] == expert_ids[None, None, :], axis=1)
        member = chosen.astype(BF16)
        place = dot(earlier, member).astype(jnp.int32)
        dispatch = (
            (place[:, :, None] == jnp.arange(capacity, dtype=jnp.int32)[None, None, :])
            & chosen[:, :, None]
        ).astype(BF16)
        return chosen, member, dispatch.reshape(rows, slots)

    chosen, member, dispatch = routing(routes)

    def slots_of(dispatch, block):
        sent = dot(dispatch, block, ((0,), (0,))).astype(BF16)
        return sent.reshape(experts, capacity, width)

    def upstream_sent(member, dispatch, block):
        choices = dot(member, dispatch, ((0,), (0,))).astype(BF16)
        choices = jnp.transpose(choices.reshape(experts, experts, capacity), (1, 0, 2))
        choices = jnp.pad(choices, ((0, 0), (0, 0), (0, width - capacity)))
        return jnp.concatenate([slots_of(dispatch, block), choices], axis=1)

    partner = count // 2

    def head_rows(weight):
        whole = jnp.pad(weight, ((0, 0), (0, extra * size)))
        return lax.dynamic_slice_in_dim(whole, here * held, held, 1).T

    head_weights = jnp.stack([head_rows(w) for w in (w_query, w_key, w_value)])

    own_sent, head_weights = after(
        (upstream_sent(member, dispatch, cotangent), head_weights), token_parts[-1][1]
    )
    upstream_slots = to_experts(own_sent)
    sequence = in_order(token_parts, "context")
    cotangent_other, routes_other = after((cotangent, routes.T), sequence)
    cotangent_other = swap(cotangent_other, "context", partner)
    routes_other = swap(routes_other, "context", partner)

    bucket_match = (
        bucket_ids[:, None] == jnp.arange(buckets, dtype=jnp.int32)[None, :]
    ).astype(F32)
    per_distance = lax.dot_general(
        jnp.pad(bias_table, ((0, 0), (0, extra))), bucket_match, (((0,), (1,)), ((), ())),
        precision=HIGHEST,
    )
    bias = jnp.pad(
        lax.dynamic_slice_in_dim(per_distance, here * group, group, 0),
        ((0, 0), (rows, 0)),
        constant_values=MASKED,
    )[:, None, :]
    normed, qkv, mixed_parts, exact, log_total = attend(
        sequence, gain_attn[None, :], head_weights, bias, count
    )
    mixed_parts, upstream_slots, cotangent_other, routes_other = lax.optimization_barrier(
        (mixed_parts, upstream_slots, cotangent_other, routes_other)
    )
    unused, member_other, dispatch_other = routing(routes_other.T)
    upstream_other = to_experts(upstream_sent(member_other, dispatch_other, cotangent_other))
    mixed = context_steps(mixed_parts).reshape(count * held, rows)[:width]
    source = tokens.astype(F32)
    middle = source + dot(mixed, w_proj, ((0,), (0,)))
    moe_normal, moe_scale = normalize(middle, gain_moe)
    routed = moe_normal.astype(BF16)

    logits = dot(routed, w_router)
    gates = chosen_softmax(logits, chosen, 1)

    def gates_of(received, upstream):
        choices = jnp.moveaxis(upstream[:, capacity:, :capacity], 1, 0) > 0.5
        slot_logits = dot(w_router, received, ((0,), (1,))).reshape(experts, lanes, capacity)
        slot_gates = chosen_softmax(slot_logits, choices, 0)
        return lax.dynamic_index_in_dim(slot_gates, own, 0, keepdims=False)[:, None, :]

    sent, upstream_other = lax.optimization_barrier((slots_of(dispatch, routed), upstream_other))
    received = to_experts(sent).reshape(slots, width)
    routed_other = swap(routed, "context", partner)
    received, routed_other = lax.optimization_barrier((received, routed_other))
    received_other = to_experts(slots_of(dispatch_other, routed_other)).reshape(slots, width)
    slot_gate = gates_of(received, upstream_slots)
    expert_out, row_grads = expert(received, upstream_slots, slot_gate, w_up[0], w_down[0])
    row_grads, received_other = lax.optimization_barrier((row_grads, received_other))
    row_returns = to_experts(row_grads)

    quarter = partner // 2
    mine = lax.rem(here // quarter, 2)
    first = (here // partner) * partner
    other_gate = gates_of(received_other, upstream_other)

    def gradients(start, hold):
        return expert_grads(
            after(start, hold)[None],
            received,
            received_other,
            upstream_slots,
            upstream_other,
            slot_gate,
            other_gate,
            w_up[0],
            w_down[0],
            count,
            quarter,
        )

    up_sent, down_sent = gradients(first + (1 - mine) * quarter, row_grads)
    up_kept, down_kept = gradients(first + mine * quarter, down_sent)
    row_returns, down_sent, up_kept, down_kept = lax.optimization_barrier(
        (row_returns, down_sent, up_kept, down_kept)
    )
    up_arrived = swap(up_sent, "context", quarter)
    low_bits = [1 << i for i in range(quarter.bit_length() - 1)][::-1]
    spread = dispatch.reshape(rows, experts, capacity).astype(F32)
    middle_grads, branch_grads, mixed_grads, gain_moe_grad, router_grad = token_back(
        row_returns,
        dispatch,
        gates,
        chosen.astype(F32),
        middle,
        cotangent,
        gain_moe[None, :],
        routed,
        w_router.astype(F32).T,
        w_proj,
    )
    arrivals = []
    grads_in = context_steps(
        jnp.pad(mixed_grads, ((0, extra * size), (0, 0))).reshape(count, held, rows),
        arrivals,
    )
    bits = bit_orders(lanes)
    out_returns = to_experts(after(expert_out, arrivals[0]).reshape(experts, capacity, width))
    grads_in, up_arrived = lax.optimization_barrier((grads_in, up_arrived))
    proj_part = dot(mixed, branch_grads).astype(BF16).reshape(lanes, width // lanes, width)
    proj_part = halve_sum(proj_part, "expert", bits).astype(BF16)
    proj_part = context_steps(proj_part.reshape(count, width // (lanes * count), width))
    proj_rows = jnp.sum(proj_part.astype(F32), axis=0).astype(BF16)

    grads_out, weight_grads, diagonals = attend_back(
        qkv, normed, bias, log_total, exact, grads_in
    )
    weight_grads, out_returns = lax.optimization_barrier((weight_grads, out_returns))
    table_part = jnp.dot(diagonals[:, 0, rows:], bucket_match, precision=HIGHEST)
    table_line = lax.dynamic_update_slice(
        jnp.zeros((count * group, buckets), F32), table_part, (here * group, 0)
    )[:HEADS].reshape(1, HEADS * buckets)
    table_line = jnp.pad(table_line, ((0, 0), (0, width - HEADS * buckets)))
    small = jnp.concatenate([router_grad, gain_moe_grad, table_line], axis=0)
    small = jnp.pad(small, ((0, lanes * SPARE - small.shape[0]), (0, 0))).astype(BF16)
    chunk = 3 * held // lanes
    pack = jnp.concatenate(
        [
            jnp.moveaxis(weight_grads.reshape(3, lanes, held // lanes, width), 1, 0).reshape(
                lanes, chunk, width
            ),
            small.reshape(lanes, SPARE, width),
        ],
        axis=1,
    )
    pack = halve_sum(pack, "expert", bits).astype(BF16)
    arrived = context_steps(grads_out)
    pack = jnp.concatenate([pack, proj_rows], axis=0)
    pack = in_order(ring_parts(pack[None], "context"), "context")
    pack, arrived = lax.optimization_barrier((pack, arrived))
    down_arrived = swap(after(down_sent, pack), "context", quarter)
    normed_grads = 0.0
    for j, weight in enumerate((w_query, w_key, w_value)):
        part = arrived[:, j].reshape(count * held, rows)[:width]
        normed_grads = normed_grads + dot(part, weight, ((0,), (1,)))
    attention_scale = lax.rsqrt(jnp.mean(source * source, axis=1, keepdims=True) + EPSILON)
    token_norm_grads, unused = normalize_back(normed_grads, source, attention_scale, gain_attn)
    token_grads = (middle_grads + token_norm_grads).astype(BF16)
    up_grad = after(up_kept, pack).astype(F32) + up_arrived.astype(F32)
    up_grad = halve_sum(up_grad, "context", low_bits, BF16)
    gated = (spread * gates[:, :, None]).reshape(rows, slots)
    output = middle + jnp.dot(
        gated, out_returns.reshape(slots, width).astype(F32), precision=HIGHEST
    )
    half = width // 2
    sides = (bits[:0:-1], bits[1:])
    parts = [
        double_gather(part, "expert", order[:1])
        for part, order in zip((pack[:, :, :half], pack[:, :, half:]), sides)
    ]
    parts, token_grads, up_grad, output = lax.optimization_barrier(
        (parts, token_grads, up_grad, output)
    )
    near = jnp.stack(
        [double_gather(part, "expert", order[1:]) for part, order in zip(parts, sides)]
    )
    near, down_arrived = lax.optimization_barrier((near, down_arrived))
    far = swap(near, "expert", bits[0])
    down_grad = down_kept.astype(F32) + down_arrived.astype(F32)
    down_grad = halve_sum(down_grad, "context", low_bits, BF16)
    grad_query, grad_key, grad_value, grad_proj, small, gain_attn_total = assemble(
        own[None], near, far, w_query, w_key, w_value, bits, chunk
    )
    gain_attn_total = gain_attn_total[:, 0] / gain_attn
    router_total = small[:experts].T
    gain_moe_total = small[experts]
    table_total = small[experts + 1, : HEADS * buckets].reshape(HEADS, buckets).T
    return (
        output.astype(BF16),
        token_grads,
        gain_attn_total,
        grad_query,
        grad_key,
        grad_value,
        grad_proj,
        table_total,
        gain_moe_total,
        router_total,
        up_grad[None],
        down_grad[None],
    )


def solution(mesh):
    return jax.shard_map(
        shards,
        mesh=mesh,
        in_specs=(
            P(("expert", "context"), None),
            P(),
            P(),
            P(),
            P(),
            P(),
            P(),
            P(),
            P(),
            P("expert", None, None),
            P("expert", None, None),
            P(("expert", "context"), None),
            P(),
            P(("expert", "context"), None),
        ),
        out_specs=(
            P(("expert", "context"), None),
            P(("expert", "context"), None),
            P(),
            P(),
            P(),
            P(),
            P(),
            P(),
            P(),
            P(),
            P("expert", None, "context"),
            P("expert", "context", None),
        ),
        check_vma=False,
    )
```
